32 devices in a mesh: blk: 8 (over y, x, core), src: 4 (over z).
Axes of the slice: x: 2, y: 2, z: 4, core: 2. Of those that a mesh axis runs over, the one named last changes fastest.
Arguments:
- windows: bfloat16 [512, 8192], P('blk', 'src'), may hold values from -6 to 6
- observed: bfloat16 [64, 2, 4096], P(None, None, 'src'), may hold values from -40 to 40
- pair_class: int32 [512, 512], P('blk'), may hold values from 0 to 63
- green: bfloat16 [64, 2, 4096], P(None, None, 'src'), may hold values from -6 to 6
- green_index: int32 [4, 512], P(None, 'blk'), may hold values from 0 to 63
- tile_index: int32 [4, 512], P(None, 'blk'), may hold values from 0 to 15
Outputs:
- gradient: float32 [16, 4096], P('src', 'blk')
The draws below stay inside these ranges and needn't reach their ends.
All inputs are finite; a program needn't handle non-finite values.
Results may differ from the reference program's by a relative error of at most 0.0051.
Values may be sent and summed in bfloat16 or wider, within the bound.
No kernel may reach another device: no remote copies, remote signals or barrier semaphores. Data moves between devices by JAX's collectives and lax.ppermute only.
A program may use at most 256 MiB of HBM per device.

```python
import math
import jax
import jax.numpy as jnp
from jax import lax

NT = 8192
TILE_SIDE = 64
NOBS = 64
NG = 64
NB = 4
STATIONS = 512
F = 4096
TP = 4096
TILES = 16


def with_ends(drawn, key, smallest, top_value):
    longest = drawn.shape.index(max(drawn.shape))
    spots = []
    for shift in (0, 1):
        where = [jax.random.randint(jax.random.fold_in(key, axis), (), 0, length) for axis, length in enumerate(drawn.shape)]
        where[longest] = (where[longest] + shift) % drawn.shape[longest]
        spots.append(tuple(where))
    return drawn.at[spots[0]].set(smallest).at[spots[1]].set(top_value)


def steps_of(stream_key, extent, shards, low, largest):
    gain = 1.0
    for position, shards_of in shards:
        draws = jax.random.uniform(jax.random.fold_in(jax.random.fold_in(stream_key, 6), position), (shards_of,), jnp.float32, low / len(shards), largest / len(shards))
        gain = gain * jnp.repeat(jnp.exp(draws), extent[position] // shards_of).reshape((-1,) + (1,) * (len(extent) - 1 - position))
    return gain


def normal_values(key, shape, deviation, limit, pieces=(), kind=jnp.bfloat16):
    entries = jax.random.normal(key, shape, jnp.float32) * deviation
    if len(pieces) > 0:
        entries = steps_of(key, shape, pieces, -0.22, 0.18) * entries
    return jnp.clip(entries, min=-limit, max=limit).astype(kind)


def setup_inputs(seed: int = 0) -> dict:
    streams_of = jax.random.split(jax.random.key(seed), 7)
    windows = normal_values(streams_of[0], (STATIONS, NT), 1.0, 6.0, ((0, 8), (1, 4)))
    observed = normal_values(streams_of[1], (NOBS, 2, F), (0.3 * STATIONS ** 0.5), 40.0, ((2, 4),))
    pair_class = with_ends(jax.random.randint(streams_of[2], (STATIONS, STATIONS), 0, NOBS), jax.random.fold_in(streams_of[2], 1), 0, NOBS - 1).astype(jnp.int32)
    green = normal_values(streams_of[3], (NG, 2, F), 1.0, 6.0, ((2, 4),))
    green_index = with_ends(jax.random.randint(streams_of[4], (NB, STATIONS), 0, NG), jax.random.fold_in(streams_of[4], 1), 0, NG - 1).astype(jnp.int32)
    tile_index = with_ends(jax.random.randint(streams_of[5], (NB, STATIONS), 0, TILES), jax.random.fold_in(streams_of[5], 1), 0, TILES - 1).astype(jnp.int32)
    return dict(windows=windows, observed=observed, pair_class=pair_class, green=green, green_index=green_index, tile_index=tile_index)


def dft_table(sample_ids, freq_ids, period):
    phase_index = sample_ids[:, None] * freq_ids[None, :] % period
    angle_rad = phase_index.astype(jnp.float32) * (2.0 * math.pi / period)
    amp_scale = 1.0 / math.sqrt(period)
    return jnp.stack([jnp.cos(angle_rad) * amp_scale, -jnp.sin(angle_rad) * amp_scale], axis=1).astype(jnp.bfloat16)

def mode_table(freq_ids, points, edge_cells):
    phase_index = freq_ids[:, None] % edge_cells * (points[None, :] % edge_cells) + freq_ids[:, None] // edge_cells * (points[None, :] // edge_cells)
    angle_rad = (phase_index % edge_cells).astype(jnp.float32) * (2.0 * math.pi / edge_cells)
    return jnp.concatenate([jnp.cos(angle_rad), -jnp.sin(angle_rad)], axis=0)

def reference(windows, observed, pair_class, green, green_index, tile_index):
    stations = windows.shape[0]
    freq_ids = jnp.arange(F, dtype=jnp.int32)
    table_rows = dft_table(jnp.arange(NT, dtype=jnp.int32), freq_ids, NT).reshape(NT, 2 * F)
    spectra = jnp.dot(windows, table_rows, preferred_element_type=jnp.float32).astype(jnp.bfloat16)
    widened = spectra.astype(jnp.float32)
    real_all, imag_all = (widened[:, :F], widened[:, F:])
    power_sum = lax.optimization_barrier(jnp.sum(real_all * real_all + imag_all * imag_all, axis=0))
    obs_table = observed.reshape(NOBS, 2 * F).astype(jnp.float32)
    obs_real, obs_imag = (obs_table[:, :F], obs_table[:, F:])

    def one_station(station_args):
        station_row, class_row = station_args
        grouped = jax.ops.segment_sum(widened, class_row, num_segments=NOBS)
        group_real, group_imag = (grouped[:, :F], grouped[:, F:])
        mix_real = lax.optimization_barrier(jnp.sum(obs_real * group_real - obs_imag * group_imag, axis=0))
        mix_imag = lax.optimization_barrier(jnp.sum(obs_real * group_imag + obs_imag * group_real, axis=0))
        return jnp.concatenate([station_row[:F] * power_sum - mix_real, station_row[F:] * power_sum - mix_imag]) / stations
    adjoint = lax.map(one_station, (widened, pair_class))
    adj_real, adj_imag = (adjoint[:, :F], adjoint[:, F:])
    green_bank = green.reshape(NG, 2 * F)
    picked = green_bank[green_index].astype(jnp.float32)
    pick_real, pick_imag = (picked[..., :F], picked[..., F:])
    weighted = jnp.concatenate([adj_real[None] * pick_real + adj_imag[None] * pick_imag, adj_real[None] * pick_imag - adj_imag[None] * pick_real], axis=-1).astype(jnp.bfloat16)
    summed_tiles = jax.ops.segment_sum(weighted.astype(jnp.float32).reshape(NB * stations, 2 * F), tile_index.reshape(NB * stations), num_segments=TILES)
    tile_spectra = summed_tiles * math.sqrt(TILES / (stations * NB))
    modes = mode_table(freq_ids, jnp.arange(TP, dtype=jnp.int32), TILE_SIDE)
    return jnp.dot(tile_spectra, modes, precision=lax.Precision.HIGHEST) / math.sqrt(F)
```

```python
import functools
import math

import jax
import jax.numpy as jnp
import numpy as np
from jax import lax
from jax.experimental import pallas as pl
from jax.experimental.pallas import tpu as pltpu
from jax.sharding import PartitionSpec as P

NT = 8192
TILE_SIDE = 64
TILE_DEV = 4
F = 4096
TP = 4096


def trig_pair(phase_index, period):
    angle_rad = phase_index.astype(jnp.float32) * (2.0 * math.pi / period)
    return (jnp.cos(angle_rad), jnp.sin(angle_rad))


def dft_rows(count, freq_ids, period):
    amp_scale = 1.0 / math.sqrt(period)
    local_freqs = freq_ids.shape[0]
    high_ids = jnp.arange(count // 128, dtype=jnp.int32)
    low_ids = jnp.arange(128, dtype=jnp.int32)
    high_cos, high_sin = trig_pair(high_ids[:, None] * 128 * freq_ids[None, :] % period, period)
    low_cos, low_sin = trig_pair(low_ids[:, None] * freq_ids[None, :] % period, period)
    cos_part = (
        high_cos[:, None, :] * low_cos[None] - high_sin[:, None, :] * low_sin[None]
    ).reshape(count, local_freqs)
    sin_part = (
        high_sin[:, None, :] * low_cos[None] + high_cos[:, None, :] * low_sin[None]
    ).reshape(count, local_freqs)
    return jnp.concatenate([cos_part * amp_scale, -sin_part * amp_scale], axis=1).astype(
        jnp.bfloat16
    )


def mode_table(freq_ids, points, edge_cells):
    phase_index = freq_ids[:, None] % edge_cells * (points[None, :] % edge_cells) + freq_ids[
        :, None
    ] // edge_cells * (points[None, :] // edge_cells)
    angle_rad = (phase_index % edge_cells).astype(jnp.float32) * (2.0 * math.pi / edge_cells)
    return jnp.concatenate([jnp.cos(angle_rad), -jnp.sin(angle_rad)], axis=0)


def general_body(windows, observed, pair_class, green, green_index, tile_index):
    panel_rows = windows.shape[0]
    local_freqs = observed.shape[2]
    class_count = observed.shape[0]
    src_index = lax.axis_index("src")
    blk_index = lax.axis_index("blk")
    stations = panel_rows * lax.axis_size("blk")
    freq_ids = src_index * local_freqs + jnp.arange(local_freqs, dtype=jnp.int32)
    shard_piece = lax.all_gather(windows, "src", axis=1, tiled=True)
    table_rows = dft_rows(shard_piece.shape[1], freq_ids, NT)
    spectra = jnp.dot(shard_piece, table_rows, preferred_element_type=jnp.float32).astype(
        jnp.bfloat16
    )
    class_ids = jnp.arange(class_count, dtype=jnp.int32)
    shard_piece = lax.all_gather(spectra, "blk", axis=0, tiled=True)
    widened = shard_piece.astype(jnp.float32)
    far_real = widened[:, :local_freqs]
    far_imag = widened[:, local_freqs:]
    power_sum = jnp.sum(far_real * far_real + far_imag * far_imag, axis=0)
    class_hot = (pair_class[:, :, None] == class_ids).astype(jnp.bfloat16)
    grouped = jnp.einsum("ijk,jf->ikf", class_hot, shard_piece, preferred_element_type=jnp.float32)
    power_sum, grouped = (power_sum, grouped)
    obs_table = observed.reshape(class_count, 2 * local_freqs).astype(jnp.float32)
    obs_real, obs_imag = (obs_table[:, :local_freqs], obs_table[:, local_freqs:])
    group_real, group_imag = (grouped[..., :local_freqs], grouped[..., local_freqs:])
    highest = lax.Precision.HIGHEST
    mix_real = jnp.einsum("kf,ikf->if", obs_real, group_real, precision=highest) - jnp.einsum(
        "kf,ikf->if", obs_imag, group_imag, precision=highest
    )
    mix_imag = jnp.einsum("kf,ikf->if", obs_real, group_imag, precision=highest) + jnp.einsum(
        "kf,ikf->if", obs_imag, group_real, precision=highest
    )
    own_spectra = spectra.astype(jnp.float32)
    adjoint = (
        own_spectra * jnp.concatenate([power_sum, power_sum])[None, :]
        - jnp.concatenate([mix_real, mix_imag], axis=1)
    ) / stations
    adj_real, adj_imag = (adjoint[:, :local_freqs], adjoint[:, local_freqs:])
    green_bank = green.reshape(green.shape[0], 2 * local_freqs)
    green_ids = jnp.arange(green_bank.shape[0], dtype=jnp.int32)
    pick_hot = (green_index[:, :, None] == green_ids).astype(jnp.bfloat16)
    picked = jnp.einsum(
        "npg,gf->npf", pick_hot, green_bank, preferred_element_type=jnp.bfloat16
    ).astype(jnp.float32)
    pick_real, pick_imag = (picked[..., :local_freqs], picked[..., local_freqs:])
    weighted = jnp.concatenate(
        [
            adj_real[None] * pick_real + adj_imag[None] * pick_imag,
            adj_real[None] * pick_imag - adj_imag[None] * pick_real,
        ],
        axis=-1,
    ).astype(jnp.bfloat16)
    tiles_all = TILE_DEV * lax.axis_size("src")
    tile_hot = (tile_index[:, :, None] == jnp.arange(tiles_all, dtype=jnp.int32)).astype(
        jnp.bfloat16
    )
    tile_spectra = jnp.einsum(
        "npt,npf->tf", tile_hot, weighted, preferred_element_type=jnp.float32
    ) * math.sqrt(tiles_all / (stations * green_index.shape[0]))
    summed = lax.psum(tile_spectra, "blk")
    point_share = TP // lax.axis_size("blk")
    points = blk_index * point_share + jnp.arange(point_share, dtype=jnp.int32)
    tile_image = jnp.dot(
        summed, mode_table(freq_ids, points, TILE_SIDE), precision=lax.Precision.HIGHEST
    ) / math.sqrt(F)
    return lax.psum_scatter(tile_image, "src", scatter_dimension=0, tiled=True)

LANES = 128
BOTH = ("blk", "src")
HIGHEST = lax.Precision.HIGHEST
NT_DIMS = (((1,), (1,)), ((), ()))
TN_DIMS = (((0,), (0,)), ((), ()))
VMEM_BYTES = 56 * 1024 * 1024


def split_bf16(values):
    high = values.astype(jnp.bfloat16)
    low = (values - high.astype(np.float32)).astype(jnp.bfloat16)
    return high, low


def forward_tables(n_src, n_blk):
    steps = NT // LANES
    per_src = steps // n_src
    own = np.arange(n_src)
    order = np.stack(
        [np.concatenate([(s ^ k) * per_src + np.arange(per_src) for k in range(n_src)]) for s in own]
    )
    rows = np.arange(steps)
    angle = 2 * np.pi / steps * ((rows[None, :, None] * order[:, None, :]) % steps)
    first = np.concatenate([np.cos(angle), -np.sin(angle)], axis=1).astype(np.float32)
    first = np.concatenate(split_bf16(first), axis=1)
    lanes = np.arange(LANES)
    angle = 2 * np.pi / NT * ((lanes[:, None] * lanes[None, :]) % NT)
    twiddle = np.stack([np.cos(angle), -np.sin(angle)]).astype(np.float32)
    devices = np.arange(n_src * n_blk)
    block = devices % n_src * n_blk + devices // n_src
    angle = 2 * np.pi / steps * ((block[:, None] * lanes[None, :]) % steps)
    cos, sin = np.cos(angle), np.sin(angle)
    third = np.concatenate(
        [np.concatenate([cos, sin], axis=1), np.concatenate([-sin, cos], axis=1)], axis=0
    )
    return first, twiddle, (third / math.sqrt(NT)).astype(np.float32)


def mode_tables(n_src, n_blk, scale):
    side = np.arange(TILE_SIDE)
    angle = 2 * np.pi / TILE_SIDE * ((side[:, None] * side[None, :]) % TILE_SIDE)
    cos, sin = np.cos(angle), np.sin(angle)
    low = np.zeros((2, 2, TILE_SIDE, 2, 2, TILE_SIDE))
    for parity in range(2):
        low[0, parity, :, parity, 0] = cos
        low[0, parity, :, parity, 1] = sin
        low[1, parity, :, parity, 0] = -sin
        low[1, parity, :, parity, 1] = cos
    low = low.reshape(4 * TILE_SIDE, 4 * TILE_SIDE) * scale
    devices = np.arange(n_src * n_blk)
    block = devices % n_src * n_blk + devices // n_src
    high_freqs = block[:, None] * 2 + np.arange(2)[None, :]
    angle = 2 * np.pi / TILE_SIDE * ((side[:, None, None] * high_freqs[None]) % TILE_SIDE)
    high = np.stack([np.cos(angle), -np.sin(angle)], axis=-1).reshape(
        n_blk, TILE_SIDE // n_blk, 4 * n_src * n_blk
    )
    return low.astype(np.float32), (high / math.sqrt(F)).astype(np.float32)


def spectra_kernel(n_src, *refs):
    pieces = refs[:n_src]
    first_ref, twiddle_ref, third_ref, out_ref, samples, reals, imags = refs[n_src:]
    stations, local = pieces[0].shape
    per_src = local // LANES
    steps = per_src * n_src
    count = third_ref.shape[0] // 2
    first = first_ref[lax.axis_index("src")]
    for k in range(n_src):
        for a in range(per_src):
            samples[pl.ds(k * per_src + a, stations, stride=steps), :] = pieces[k][
                :, a * LANES : (a + 1) * LANES
            ].astype(jnp.float32)
    twiddle_real, twiddle_imag = twiddle_ref[0], twiddle_ref[1]
    third = third_ref[...]
    for station in range(stations):
        rows = samples[station * steps : (station + 1) * steps, :].astype(jnp.bfloat16)
        parts = jnp.dot(first, rows, preferred_element_type=jnp.float32)
        real = parts[:steps] + parts[2 * steps : 3 * steps]
        imag = parts[steps : 2 * steps] + parts[3 * steps :]
        real = jnp.concatenate([real] * (LANES // steps), axis=0)
        imag = jnp.concatenate([imag] * (LANES // steps), axis=0)
        turned = jnp.concatenate(
            [
                real * twiddle_real - imag * twiddle_imag,
                real * twiddle_imag + imag * twiddle_real,
            ],
            axis=1,
        )
        result = lax.dot_general(
            third, turned, NT_DIMS, precision=HIGHEST, preferred_element_type=jnp.float32
        )
        reals[pl.ds(station, count, stride=stations), :] = result[:count]
        imags[pl.ds(station, count, stride=stations), :] = result[count:]
    out_ref[:, :LANES] = reals[...].astype(jnp.bfloat16)
    out_ref[:, LANES:] = imags[...].astype(jnp.bfloat16)


def adjoint_kernel(n_blk, n_src, slots, tiles, chunk, *refs):
    packs = refs[:n_blk]
    spectra_ref, observed_ref, green_ref, low_ref, out_ref, classes, picks, mixed, total = refs[
        n_blk:
    ]
    stations = spectra_ref.shape[0]
    panel = stations // n_blk
    class_count = observed_ref.shape[0]
    green_count = green_ref.shape[0]
    local_freqs = observed_ref.shape[1] // 2
    blk_index = lax.axis_index("blk")
    for k in range(n_blk):
        owner = blk_index ^ k
        at = pl.ds(pl.multiple_of(owner * panel, panel), panel)
        classes[at, :] = packs[k][:panel].astype(jnp.int32)
        picks[owner] = packs[k][panel : panel + 16, :LANES].astype(jnp.int32)
    here = pl.ds(pl.multiple_of(blk_index * LANES, LANES), LANES)
    there = pl.ds(pl.multiple_of(local_freqs + blk_index * LANES, LANES), LANES)
    obs_real = observed_ref[:, here].astype(jnp.float32)[None]
    obs_imag = observed_ref[:, there].astype(jnp.float32)[None]
    green = jnp.concatenate([green_ref[:, here], green_ref[:, there]], axis=1)
    spectra = spectra_ref[...]
    widened = spectra.astype(jnp.float32)
    power = jnp.sum(widened * widened, axis=0, keepdims=True)
    power = power[:, :LANES] + power[:, LANES:]
    power = jnp.concatenate([power, power], axis=1)
    class_ids = lax.broadcasted_iota(jnp.int32, (1, class_count, stations), 1)
    total[...] = jnp.zeros_like(total)

    def one_panel(owner, carry):
        start = pl.multiple_of(owner * panel, panel)
        for part in range(panel // chunk):
            rows = classes[pl.ds(start + part * chunk, chunk), :]
            hot = jnp.where(rows[:, None, :] == class_ids, 1.0, 0.0).astype(jnp.bfloat16)
            grouped = jnp.dot(
                hot.reshape(chunk * class_count, stations),
                spectra,
                preferred_element_type=jnp.float32,
            ).reshape(chunk, class_count, 2 * LANES)
            group_real, group_imag = grouped[..., :LANES], grouped[..., LANES:]
            at = pl.ds(part * chunk, chunk)
            mixed[at, :LANES] = jnp.sum(obs_real * group_real - obs_imag * group_imag, axis=1)
            mixed[at, LANES:] = jnp.sum(obs_real * group_imag + obs_imag * group_real, axis=1)
        own = spectra_ref[pl.ds(start, panel), :].astype(jnp.float32)
        adjoint = (own * power - mixed[...]) * (1.0 / stations)
        adj_real, adj_imag = adjoint[:, :LANES], adjoint[:, LANES:]
        ids = picks[owner]
        green_ids = lax.broadcasted_iota(jnp.int32, (green_count, panel), 0)
        tile_ids = lax.broadcasted_iota(jnp.int32, (tiles, panel), 0)
        for slot in range(slots):
            pick = jnp.where(ids[slot : slot + 1, :panel] == green_ids, 1.0, 0.0)
            tile = jnp.where(ids[8 + slot : 9 + slot, :panel] == tile_ids, 1.0, 0.0)
            picked = lax.dot_general(
                pick.astype(jnp.bfloat16), green, TN_DIMS, preferred_element_type=jnp.float32
            )
            pick_real, pick_imag = picked[:, :LANES], picked[:, LANES:]
            weighted = jnp.concatenate(
                [
                    adj_real * pick_real + adj_imag * pick_imag,
                    adj_real * pick_imag - adj_imag * pick_real,
                ],
                axis=1,
            ).astype(jnp.bfloat16)
            total[...] += jnp.dot(
                tile.astype(jnp.bfloat16), weighted, preferred_element_type=jnp.float32
            )
        return carry

    lax.fori_loop(0, n_blk, one_panel, 0)
    low = jnp.dot(
        total[...], low_ref[...], precision=HIGHEST, preferred_element_type=jnp.float32
    )
    share = tiles // n_src
    rows = []
    for owner in range(n_src):
        for part in range(4):
            piece = low[owner * share : (owner + 1) * share, part * TILE_SIDE : (part + 1) * TILE_SIDE]
            rows.append(jnp.concatenate([piece[t : t + 1] for t in range(share)], axis=1))
    rows = jnp.concatenate(rows, axis=0)
    for copy in range(n_blk):
        out_ref[copy * 4 * n_src : (copy + 1) * 4 * n_src, :] = rows


def image_kernel(high_ref, parts_ref, out_ref):
    high = high_ref[lax.axis_index("blk")]
    image = jnp.dot(
        high, parts_ref[...], precision=HIGHEST, preferred_element_type=jnp.float32
    )
    rows = high.shape[0]
    for tile in range(out_ref.shape[0]):
        for row in range(rows):
            out_ref[tile : tile + 1, row * TILE_SIDE : (row + 1) * TILE_SIDE] = image[
                row : row + 1, tile * TILE_SIDE : (tile + 1) * TILE_SIDE
            ]


def swap(values, axis, distance):
    size = lax.axis_size(axis)
    return lax.ppermute(values, axis, [(i, i ^ distance) for i in range(size)])


def split_body(windows, observed, pair_class, green, green_index, tile_index):
    n_blk, n_src = lax.axis_size("blk"), lax.axis_size("src")
    src_index = lax.axis_index("src")
    panel, local = windows.shape
    stations = panel * n_blk
    slots = green_index.shape[0]
    tiles = TILE_DEV * n_src
    share = panel // n_src
    pieces = [
        lax.dynamic_slice_in_dim(windows, (src_index ^ k) * share, share, 0) for k in range(n_src)
    ]
    pieces = [pieces[0]] + [swap(pieces[k], "src", k) for k in range(1, n_src)]

    def widen(ids):
        return jnp.pad(ids, ((0, 8 - slots), (0, stations - panel)))

    pack = jnp.concatenate([pair_class, widen(green_index), widen(tile_index)], axis=0).astype(
        jnp.bfloat16
    )
    packs = [pack] + [swap(pack, "blk", k) for k in range(1, n_blk)]

    first, twiddle, third = forward_tables(n_src, n_blk)
    low, high = mode_tables(n_src, n_blk, math.sqrt(tiles / (stations * slots)))
    devices = n_blk * n_src
    params = pltpu.CompilerParams(vmem_limit_bytes=VMEM_BYTES)
    blocks = pl.pallas_call(
        functools.partial(spectra_kernel, n_src),
        out_shape=jax.ShapeDtypeStruct((devices * share, 2 * LANES), jnp.bfloat16),
        scratch_shapes=[
            pltpu.VMEM((share * NT // LANES, LANES), jnp.float32),
            pltpu.VMEM((devices * share, LANES), jnp.float32),
            pltpu.VMEM((devices * share, LANES), jnp.float32),
        ],
        compiler_params=params,
        name="spectra",
    )(*pieces, first, twiddle, third)
    spectra = lax.all_to_all(
        blocks.reshape(devices, share, 2 * LANES), BOTH, 0, 0, tiled=True
    ).reshape(stations, 2 * LANES)
    class_count = observed.shape[0]
    parts = pl.pallas_call(
        functools.partial(adjoint_kernel, n_blk, n_src, slots, tiles, 8),
        out_shape=jax.ShapeDtypeStruct((4 * devices, TILE_DEV * TILE_SIDE), jnp.float32),
        scratch_shapes=[
            pltpu.VMEM((stations, stations), jnp.int32),
            pltpu.VMEM((n_blk, 16, LANES), jnp.int32),
            pltpu.VMEM((panel, 2 * LANES), jnp.float32),
            pltpu.VMEM((tiles, 2 * LANES), jnp.float32),
        ],
        compiler_params=params,
        name="adjoint",
    )(
        *packs,
        spectra,
        observed.reshape(class_count, -1),
        green.reshape(green.shape[0], -1),
        low,
    )
    parts = lax.all_to_all(
        parts.reshape(devices, 4, TILE_DEV * TILE_SIDE), BOTH, 0, 0, tiled=True
    ).reshape(4 * devices, TILE_DEV * TILE_SIDE)
    return pl.pallas_call(
        image_kernel,
        out_shape=jax.ShapeDtypeStruct((TILE_DEV, TP // n_blk), jnp.float32),
        compiler_params=params,
        name="image",
    )(high, parts)


def solution(mesh):
    in_specs = (
        P("blk", "src"),
        P(None, None, "src"),
        P("blk", None),
        P(None, None, "src"),
        P(None, "blk"),
        P(None, "blk"),
    )
    out_specs = P("src", "blk")
    whole_lanes = mesh.size * LANES == F
    body = split_body if whole_lanes else general_body
    return jax.shard_map(body, mesh=mesh, in_specs=in_specs, out_specs=out_specs, check_vma=False)
```

```python
import functools
import math

import jax
import jax.numpy as jnp
import numpy as np
from jax import lax
from jax.experimental import pallas as pl
from jax.experimental.pallas import tpu as pltpu
from jax.sharding import PartitionSpec as P

NT = 8192
TILE_SIDE = 64
TILE_DEV = 4
F = 4096
TP = 4096


def trig_pair(phase_index, period):
    angle_rad = phase_index.astype(jnp.float32) * (2.0 * math.pi / period)
    return (jnp.cos(angle_rad), jnp.sin(angle_rad))


def dft_rows(count, freq_ids, period):
    amp_scale = 1.0 / math.sqrt(period)
    local_freqs = freq_ids.shape[0]
    high_ids = jnp.arange(count // 128, dtype=jnp.int32)
    low_ids = jnp.arange(128, dtype=jnp.int32)
    high_cos, high_sin = trig_pair(high_ids[:, None] * 128 * freq_ids[None, :] % period, period)
    low_cos, low_sin = trig_pair(low_ids[:, None] * freq_ids[None, :] % period, period)
    cos_part = (
        high_cos[:, None, :] * low_cos[None] - high_sin[:, None, :] * low_sin[None]
    ).reshape(count, local_freqs)
    sin_part = (
        high_sin[:, None, :] * low_cos[None] + high_cos[:, None, :] * low_sin[None]
    ).reshape(count, local_freqs)
    return jnp.concatenate([cos_part * amp_scale, -sin_part * amp_scale], axis=1).astype(
        jnp.bfloat16
    )


def mode_table(freq_ids, points, edge_cells):
    phase_index = freq_ids[:, None] % edge_cells * (points[None, :] % edge_cells) + freq_ids[
        :, None
    ] // edge_cells * (points[None, :] // edge_cells)
    angle_rad = (phase_index % edge_cells).astype(jnp.float32) * (2.0 * math.pi / edge_cells)
    return jnp.concatenate([jnp.cos(angle_rad), -jnp.sin(angle_rad)], axis=0)


def general_body(windows, observed, pair_class, green, green_index, tile_index):
    panel_rows = windows.shape[0]
    local_freqs = observed.shape[2]
    class_count = observed.shape[0]
    src_index = lax.axis_index("src")
    blk_index = lax.axis_index("blk")
    stations = panel_rows * lax.axis_size("blk")
    freq_ids = src_index * local_freqs + jnp.arange(local_freqs, dtype=jnp.int32)
    shard_piece = lax.all_gather(windows, "src", axis=1, tiled=True)
    table_rows = dft_rows(shard_piece.shape[1], freq_ids, NT)
    spectra = jnp.dot(shard_piece, table_rows, preferred_element_type=jnp.float32).astype(
        jnp.bfloat16
    )
    class_ids = jnp.arange(class_count, dtype=jnp.int32)
    shard_piece = lax.all_gather(spectra, "blk", axis=0, tiled=True)
    widened = shard_piece.astype(jnp.float32)
    far_real = widened[:, :local_freqs]
    far_imag = widened[:, local_freqs:]
    power_sum = jnp.sum(far_real * far_real + far_imag * far_imag, axis=0)
    class_hot = (pair_class[:, :, None] == class_ids).astype(jnp.bfloat16)
    grouped = jnp.einsum("ijk,jf->ikf", class_hot, shard_piece, preferred_element_type=jnp.float32)
    power_sum, grouped = (power_sum, grouped)
    obs_table = observed.reshape(class_count, 2 * local_freqs).astype(jnp.float32)
    obs_real, obs_imag = (obs_table[:, :local_freqs], obs_table[:, local_freqs:])
    group_real, group_imag = (grouped[..., :local_freqs], grouped[..., local_freqs:])
    highest = lax.Precision.HIGHEST
    mix_real = jnp.einsum("kf,ikf->if", obs_real, group_real, precision=highest) - jnp.einsum(
        "kf,ikf->if", obs_imag, group_imag, precision=highest
    )
    mix_imag = jnp.einsum("kf,ikf->if", obs_real, group_imag, precision=highest) + jnp.einsum(
        "kf,ikf->if", obs_imag, group_real, precision=highest
    )
    own_spectra = spectra.astype(jnp.float32)
    adjoint = (
        own_spectra * jnp.concatenate([power_sum, power_sum])[None, :]
        - jnp.concatenate([mix_real, mix_imag], axis=1)
    ) / stations
    adj_real, adj_imag = (adjoint[:, :local_freqs], adjoint[:, local_freqs:])
    green_bank = green.reshape(green.shape[0], 2 * local_freqs)
    green_ids = jnp.arange(green_bank.shape[0], dtype=jnp.int32)
    pick_hot = (green_index[:, :, None] == green_ids).astype(jnp.bfloat16)
    picked = jnp.einsum(
        "npg,gf->npf", pick_hot, green_bank, preferred_element_type=jnp.bfloat16
    ).astype(jnp.float32)
    pick_real, pick_imag = (picked[..., :local_freqs], picked[..., local_freqs:])
    weighted = jnp.concatenate(
        [
            adj_real[None] * pick_real + adj_imag[None] * pick_imag,
            adj_real[None] * pick_imag - adj_imag[None] * pick_real,
        ],
        axis=-1,
    ).astype(jnp.bfloat16)
    tiles_all = TILE_DEV * lax.axis_size("src")
    tile_hot = (tile_index[:, :, None] == jnp.arange(tiles_all, dtype=jnp.int32)).astype(
        jnp.bfloat16
    )
    tile_spectra = jnp.einsum(
        "npt,npf->tf", tile_hot, weighted, preferred_element_type=jnp.float32
    ) * math.sqrt(tiles_all / (stations * green_index.shape[0]))
    summed = lax.psum(tile_spectra, "blk")
    point_share = TP // lax.axis_size("blk")
    points = blk_index * point_share + jnp.arange(point_share, dtype=jnp.int32)
    tile_image = jnp.dot(
        summed, mode_table(freq_ids, points, TILE_SIDE), precision=lax.Precision.HIGHEST
    ) / math.sqrt(F)
    return lax.psum_scatter(tile_image, "src", scatter_dimension=0, tiled=True)

LANES = 128
BOTH = ("blk", "src")
HIGHEST = lax.Precision.HIGHEST
NT_DIMS = (((1,), (1,)), ((), ()))
TN_DIMS = (((0,), (0,)), ((), ()))
VMEM_BYTES = 56 * 1024 * 1024
PARTS_TYPE = jnp.bfloat16


def split_bf16(values):
    high = values.astype(jnp.bfloat16)
    low = (values - high.astype(np.float32)).astype(jnp.bfloat16)
    return high, low


def forward_tables(n_src, n_blk):
    steps = NT // LANES
    per_src = steps // n_src
    own = np.arange(n_src)
    order = np.stack(
        [np.concatenate([(s ^ k) * per_src + np.arange(per_src) for k in range(n_src)]) for s in own]
    )
    rows = np.arange(steps)
    angle = 2 * np.pi / steps * ((rows[None, :, None] * order[:, None, :]) % steps)
    first = np.concatenate([np.cos(angle), -np.sin(angle)], axis=1).astype(np.float32)
    first = np.concatenate(split_bf16(first), axis=1)
    lanes = np.arange(LANES)
    angle = 2 * np.pi / NT * ((lanes[:, None] * lanes[None, :]) % NT)
    twiddle = np.stack([np.cos(angle), -np.sin(angle)]).astype(np.float32)
    devices = np.arange(n_src * n_blk)
    block = devices % n_src * n_blk + devices // n_src
    angle = 2 * np.pi / steps * ((block[:, None] * lanes[None, :]) % steps)
    cos, sin = np.cos(angle), np.sin(angle)
    third = np.concatenate(
        [np.concatenate([cos, sin], axis=1), np.concatenate([-sin, cos], axis=1)], axis=0
    )
    third = split_bf16((third / math.sqrt(NT)).astype(np.float32))
    return first, twiddle, np.concatenate(third, axis=0)


def mode_tables(n_src, n_blk, scale):
    side = np.arange(TILE_SIDE)
    angle = 2 * np.pi / TILE_SIDE * ((side[:, None] * side[None, :]) % TILE_SIDE)
    cos, sin = np.cos(angle), np.sin(angle)
    low = np.zeros((2, 2, TILE_SIDE, 2, 2, TILE_SIDE))
    for parity in range(2):
        low[0, parity, :, parity, 0] = cos
        low[0, parity, :, parity, 1] = sin
        low[1, parity, :, parity, 0] = -sin
        low[1, parity, :, parity, 1] = cos
    low = low.reshape(4 * TILE_SIDE, 4 * TILE_SIDE) * scale
    devices = np.arange(n_src * n_blk)
    block = np.stack(
        [devices % n_src * n_blk + ((devices // n_src) ^ other) for other in range(2)], axis=1
    )
    high_freqs = block[..., None] * 2 + np.arange(2)
    angle = 2 * np.pi / TILE_SIDE * ((side[:, None, None, None] * high_freqs[None]) % TILE_SIDE)
    part = np.stack([np.cos(angle), -np.sin(angle)], axis=-1).reshape(
        n_blk, TILE_SIDE // n_blk, n_src * n_blk, 2, 4
    )
    high = np.zeros((n_blk, 2, TILE_SIDE // n_blk, n_src * n_blk, 2, 2, 4))
    for half in range(2):
        high[:, half, :, :, :, half] = part
    high = high.reshape(n_blk, 2 * TILE_SIDE // n_blk, 16 * n_src * n_blk)
    return low.astype(np.float32), (high / math.sqrt(F)).astype(np.float32)


def spectra_kernel(n_src, *refs):
    pieces = refs[:n_src]
    first_ref, twiddle_ref, third_ref, out_ref, samples, reals, imags = refs[n_src:]
    stations, local = pieces[0].shape
    per_src = local // LANES
    steps = per_src * n_src
    count = third_ref.shape[0] // 4
    first = first_ref[lax.axis_index("src")]
    for k in range(n_src):
        for a in range(per_src):
            samples[pl.ds(k * per_src + a, stations, stride=steps), :] = pieces[k][
                :, a * LANES : (a + 1) * LANES
            ].astype(jnp.float32)
    twiddle_real, twiddle_imag = twiddle_ref[0], twiddle_ref[1]
    third = third_ref[...]
    for station in range(0, stations, 2):
        rows = jnp.concatenate(
            [samples[(station + h) * steps : (station + h + 1) * steps, :] for h in range(2)], axis=1
        ).astype(jnp.bfloat16)
        parts = jnp.dot(first, rows, preferred_element_type=jnp.float32)
        reals_here = parts[:steps] + parts[2 * steps : 3 * steps]
        imags_here = parts[steps : 2 * steps] + parts[3 * steps :]
        turned = []
        for h in range(2):
            at = slice(h * LANES, (h + 1) * LANES)
            real = jnp.concatenate([reals_here[:, at]] * (LANES // steps), axis=0)
            imag = jnp.concatenate([imags_here[:, at]] * (LANES // steps), axis=0)
            turned.append(
                jnp.concatenate(
                    [
                        real * twiddle_real - imag * twiddle_imag,
                        real * twiddle_imag + imag * twiddle_real,
                    ],
                    axis=1,
                )
            )
        turned = jnp.concatenate(turned, axis=0)
        high = turned.astype(jnp.bfloat16)
        low = (turned - high.astype(jnp.float32)).astype(jnp.bfloat16)
        result = lax.dot_general(third, high, NT_DIMS, preferred_element_type=jnp.float32)
        result = (
            result[: 2 * count]
            + result[2 * count :]
            + lax.dot_general(
                third[: 2 * count], low, NT_DIMS, preferred_element_type=jnp.float32
            )
        )
        for h in range(2):
            at = slice(h * LANES, (h + 1) * LANES)
            reals[pl.ds(station + h, count, stride=stations), :] = result[:count, at]
            imags[pl.ds(station + h, count, stride=stations), :] = result[count:, at]
    out_ref[:, :LANES] = reals[...].astype(jnp.bfloat16)
    out_ref[:, LANES:] = imags[...].astype(jnp.bfloat16)


def adjoint_kernel(panels, slots, n_src, chunk, *refs):
    packs = refs[:panels]
    observed_ref, green_ref, spectra_ref, other_ref, low_ref, out_ref = refs[panels : panels + 6]
    spectra, classes, numbers, bank, green, mixed, total = refs[panels + 6 :]
    stations = spectra_ref.shape[0]
    panel = classes.shape[0] // panels
    class_count = bank.shape[0]
    tiles = total.shape[0]
    blk_index = lax.axis_index("blk")
    for other in range(2):
        at = pl.ds(pl.multiple_of((blk_index ^ other) * LANES, LANES), LANES)
        lanes = slice(2 * other * LANES, 2 * (other + 1) * LANES)
        pair = observed_ref[:, :, at].astype(jnp.float32)
        bank[:, lanes] = jnp.concatenate([pair[:, 0, :], pair[:, 1, :]], axis=1)
        pair = green_ref[:, :, at].astype(jnp.float32)
        pair = jnp.concatenate([pair[:, 0, :], pair[:, 1, :]], axis=1)
        green[:, lanes] = pair.astype(jnp.bfloat16)
    for k, pack in enumerate(packs):
        classes[k * panel : (k + 1) * panel, :] = pack[:panel].astype(jnp.int32)
        ids = pack[panel : panel + 16, :LANES].astype(jnp.int32)
        for row in range(2):
            numbers[k, row : row + 1] = jnp.concatenate(
                [ids[8 * row + slot : 8 * row + slot + 1, :panel] for slot in range(slots)], axis=1
            )
    spectra[:, : 2 * LANES] = spectra_ref[...]
    spectra[:, 2 * LANES :] = other_ref[...]
    widened = spectra[...].astype(jnp.float32)
    squares = jnp.sum(widened * widened, axis=0, keepdims=True)
    lanes = [slice(part * LANES, (part + 1) * LANES) for part in range(4)]
    power = []
    for real, imag in (lanes[:2], lanes[2:]):
        power += [squares[:, real] + squares[:, imag]] * 2
    power = jnp.concatenate(power, axis=1)
    green_ids = lax.broadcasted_iota(jnp.int32, (green.shape[0], slots * panel), 0)
    tile_ids = lax.broadcasted_iota(jnp.int32, (tiles, slots * panel), 0)
    class_ids = lax.broadcasted_iota(jnp.int32, (1, class_count, stations), 1)
    total[...] = jnp.zeros_like(total)

    def mix(place):
        start = pl.multiple_of(place * panel, panel)
        for part in range(panel // chunk):
            at = pl.ds(start + part * chunk, chunk)
            hot = jnp.where(classes[at, :][:, None, :] == class_ids, 1.0, 0.0)
            grouped = jnp.dot(
                hot.astype(jnp.bfloat16).reshape(chunk * class_count, stations),
                spectra[...],
                preferred_element_type=jnp.float32,
            ).reshape(chunk, class_count, 4 * LANES)
            for real, imag in (lanes[:2], lanes[2:]):
                obs_real, obs_imag = bank[:, real][None], bank[:, imag][None]
                group_real, group_imag = grouped[..., real], grouped[..., imag]
                mixed[at, real] = jnp.sum(obs_real * group_real - obs_imag * group_imag, axis=1)
                mixed[at, imag] = jnp.sum(obs_real * group_imag + obs_imag * group_real, axis=1)

    def gather(place):
        at = pl.ds(pl.multiple_of(place * panel, panel), panel)
        owner = blk_index ^ (2 * place)
        own = spectra[pl.ds(pl.multiple_of(owner * panel, panel), panel), :].astype(jnp.float32)
        adjoint = (own * power - mixed[at, :]) * (1.0 / stations)
        ids = numbers[place]
        pick = jnp.where(ids[:1] == green_ids, 1.0, 0.0).astype(jnp.bfloat16)
        tile = jnp.where(ids[1:2] == tile_ids, 1.0, 0.0).astype(jnp.bfloat16)
        all_picked = lax.dot_general(
            pick, green[...], TN_DIMS, preferred_element_type=jnp.float32
        )
        weighted = []
        for slot in range(slots):
            picked = all_picked[slot * panel : (slot + 1) * panel]
            row = []
            for real, imag in (lanes[:2], lanes[2:]):
                row.append(adjoint[:, real] * picked[:, real] + adjoint[:, imag] * picked[:, imag])
                row.append(adjoint[:, real] * picked[:, imag] - adjoint[:, imag] * picked[:, real])
            weighted.append(jnp.concatenate(row, axis=1).astype(jnp.bfloat16))
        total[...] += jnp.dot(
            tile,
            jnp.concatenate(weighted, axis=0),
            preferred_element_type=jnp.float32,
        )

    mix(0)

    def one_panel(place, carry):
        gather(place - 1)
        mix(place)
        return carry

    lax.fori_loop(1, panels, one_panel, 0)
    gather(panels - 1)
    low = [
        jnp.dot(
            total[:, at], low_ref[...], precision=HIGHEST, preferred_element_type=jnp.float32
        )
        for at in (slice(0, 2 * LANES), slice(2 * LANES, 4 * LANES))
    ]
    rows = []
    for owner in range(n_src):
        for other in range(2):
            for half in range(2):
                at = owner * (tiles // n_src) + 2 * half
                for part in range(4):
                    side = slice(part * TILE_SIDE, (part + 1) * TILE_SIDE)
                    rows.append(
                        jnp.concatenate(
                            [low[other][at : at + 1, side], low[other][at + 1 : at + 2, side]], axis=1
                        )
                    )
    rows = jnp.concatenate(rows, axis=0).astype(out_ref.dtype)
    for copy in range(out_ref.shape[0] // rows.shape[0]):
        out_ref[copy * 16 * n_src : (copy + 1) * 16 * n_src, :] = rows


def image_kernel(high_ref, parts_ref, out_ref):
    high = high_ref[lax.axis_index("blk")]
    image = jnp.dot(
        high,
        parts_ref[...].astype(jnp.float32),
        precision=HIGHEST,
        preferred_element_type=jnp.float32,
    )
    rows = high.shape[0] // 2
    for tile in range(out_ref.shape[0]):
        half, side = tile // 2, tile % 2
        for row in range(rows):
            at = half * rows + row
            out_ref[tile : tile + 1, row * TILE_SIDE : (row + 1) * TILE_SIDE] = image[
                at : at + 1, side * TILE_SIDE : (side + 1) * TILE_SIDE
            ]


def swap(values, axis, distance):
    size = lax.axis_size(axis)
    return lax.ppermute(values, axis, [(i, i ^ distance) for i in range(size)])


def split_body(windows, observed, pair_class, green, green_index, tile_index):
    n_blk, n_src = lax.axis_size("blk"), lax.axis_size("src")
    src_index = lax.axis_index("src")
    panel, local = windows.shape
    stations = panel * n_blk
    slots = green_index.shape[0]
    tiles = TILE_DEV * n_src
    share = panel // n_src
    pieces = [
        lax.dynamic_slice_in_dim(windows, (src_index ^ k) * share, share, 0) for k in range(n_src)
    ]
    pieces = [pieces[0]] + [swap(pieces[k], "src", k) for k in range(1, n_src)]

    def widen(ids):
        return jnp.pad(ids, ((0, 8 - slots), (0, stations - panel)))

    pack = jnp.concatenate([pair_class, widen(green_index), widen(tile_index)], axis=0).astype(
        jnp.bfloat16
    )
    packs = [pack] + [swap(pack, "blk", k) for k in range(2, n_blk, 2)]

    first, twiddle, third = forward_tables(n_src, n_blk)
    low, high = mode_tables(n_src, n_blk, math.sqrt(tiles / (stations * slots)))
    devices = n_blk * n_src
    params = pltpu.CompilerParams(vmem_limit_bytes=VMEM_BYTES)
    blocks = pl.pallas_call(
        functools.partial(spectra_kernel, n_src),
        out_shape=jax.ShapeDtypeStruct((devices * share, 2 * LANES), jnp.bfloat16),
        scratch_shapes=[
            pltpu.VMEM((share * NT // LANES, LANES), jnp.float32),
            pltpu.VMEM((devices * share, LANES), jnp.float32),
            pltpu.VMEM((devices * share, LANES), jnp.float32),
        ],
        compiler_params=params,
        name="spectra",
    )(*pieces, first, twiddle, third)
    spectra = lax.all_to_all(
        blocks.reshape(devices, share, 2 * LANES), BOTH, 0, 0, tiled=True
    ).reshape(stations, 2 * LANES)
    class_count = observed.shape[0]
    panels = n_blk // 2
    spectra, packs = lax.optimization_barrier((spectra, packs))
    parts = pl.pallas_call(
        functools.partial(adjoint_kernel, panels, slots, n_src, 8),
        out_shape=jax.ShapeDtypeStruct((16 * devices, 2 * TILE_SIDE), PARTS_TYPE),
        scratch_shapes=[
            pltpu.VMEM((stations, 4 * LANES), jnp.bfloat16),
            pltpu.VMEM((panels * panel, stations), jnp.int32),
            pltpu.VMEM((panels, 8, slots * panel), jnp.int32),
            pltpu.VMEM((class_count, 4 * LANES), jnp.float32),
            pltpu.VMEM((green.shape[0], 4 * LANES), jnp.bfloat16),
            pltpu.VMEM((panels * panel, 4 * LANES), jnp.float32),
            pltpu.VMEM((tiles, 4 * LANES), jnp.float32),
        ],
        compiler_params=params,
        name="adjoint",
    )(*packs, observed, green, spectra, swap(spectra, "blk", 1), low)
    parts = lax.all_to_all(
        parts.reshape(devices, 16, 2 * TILE_SIDE), BOTH, 0, 0, tiled=True
    ).reshape(16 * devices, 2 * TILE_SIDE)
    return pl.pallas_call(
        image_kernel,
        out_shape=jax.ShapeDtypeStruct((TILE_DEV, TP // n_blk), jnp.float32),
        compiler_params=params,
        name="image",
    )(high, parts)


def solution(mesh):
    in_specs = (
        P("blk", "src"),
        P(None, None, "src"),
        P("blk", None),
        P(None, None, "src"),
        P(None, "blk"),
        P(None, "blk"),
    )
    out_specs = P("src", "blk")
    whole_lanes = mesh.size * LANES == F
    body = split_body if whole_lanes else general_body
    return jax.shard_map(body, mesh=mesh, in_specs=in_specs, out_specs=out_specs, check_vma=False)
```

```python
import functools
import math

import jax
import jax.numpy as jnp
import numpy as np
from jax import lax
from jax.experimental import pallas as pl
from jax.experimental.pallas import tpu as pltpu
from jax.sharding import PartitionSpec as P

NT = 8192
TILE_SIDE = 64
TILE_DEV = 4
F = 4096
TP = 4096


def trig_pair(phase_index, period):
    angle_rad = phase_index.astype(jnp.float32) * (2.0 * math.pi / period)
    return (jnp.cos(angle_rad), jnp.sin(angle_rad))


def dft_rows(count, freq_ids, period):
    amp_scale = 1.0 / math.sqrt(period)
    local_freqs = freq_ids.shape[0]
    high_ids = jnp.arange(count // 128, dtype=jnp.int32)
    low_ids = jnp.arange(128, dtype=jnp.int32)
    high_cos, high_sin = trig_pair(high_ids[:, None] * 128 * freq_ids[None, :] % period, period)
    low_cos, low_sin = trig_pair(low_ids[:, None] * freq_ids[None, :] % period, period)
    cos_part = (
        high_cos[:, None, :] * low_cos[None] - high_sin[:, None, :] * low_sin[None]
    ).reshape(count, local_freqs)
    sin_part = (
        high_sin[:, None, :] * low_cos[None] + high_cos[:, None, :] * low_sin[None]
    ).reshape(count, local_freqs)
    return jnp.concatenate([cos_part * amp_scale, -sin_part * amp_scale], axis=1).astype(
        jnp.bfloat16
    )


def mode_table(freq_ids, points, edge_cells):
    phase_index = freq_ids[:, None] % edge_cells * (points[None, :] % edge_cells) + freq_ids[
        :, None
    ] // edge_cells * (points[None, :] // edge_cells)
    angle_rad = (phase_index % edge_cells).astype(jnp.float32) * (2.0 * math.pi / edge_cells)
    return jnp.concatenate([jnp.cos(angle_rad), -jnp.sin(angle_rad)], axis=0)


def general_body(windows, observed, pair_class, green, green_index, tile_index):
    panel_rows = windows.shape[0]
    local_freqs = observed.shape[2]
    class_count = observed.shape[0]
    src_index = lax.axis_index("src")
    blk_index = lax.axis_index("blk")
    stations = panel_rows * lax.axis_size("blk")
    freq_ids = src_index * local_freqs + jnp.arange(local_freqs, dtype=jnp.int32)
    shard_piece = lax.all_gather(windows, "src", axis=1, tiled=True)
    table_rows = dft_rows(shard_piece.shape[1], freq_ids, NT)
    spectra = jnp.dot(shard_piece, table_rows, preferred_element_type=jnp.float32).astype(
        jnp.bfloat16
    )
    class_ids = jnp.arange(class_count, dtype=jnp.int32)
    shard_piece = lax.all_gather(spectra, "blk", axis=0, tiled=True)
    widened = shard_piece.astype(jnp.float32)
    far_real = widened[:, :local_freqs]
    far_imag = widened[:, local_freqs:]
    power_sum = jnp.sum(far_real * far_real + far_imag * far_imag, axis=0)
    class_hot = (pair_class[:, :, None] == class_ids).astype(jnp.bfloat16)
    grouped = jnp.einsum("ijk,jf->ikf", class_hot, shard_piece, preferred_element_type=jnp.float32)
    power_sum, grouped = (power_sum, grouped)
    obs_table = observed.reshape(class_count, 2 * local_freqs).astype(jnp.float32)
    obs_real, obs_imag = (obs_table[:, :local_freqs], obs_table[:, local_freqs:])
    group_real, group_imag = (grouped[..., :local_freqs], grouped[..., local_freqs:])
    highest = lax.Precision.HIGHEST
    mix_real = jnp.einsum("kf,ikf->if", obs_real, group_real, precision=highest) - jnp.einsum(
        "kf,ikf->if", obs_imag, group_imag, precision=highest
    )
    mix_imag = jnp.einsum("kf,ikf->if", obs_real, group_imag, precision=highest) + jnp.einsum(
        "kf,ikf->if", obs_imag, group_real, precision=highest
    )
    own_spectra = spectra.astype(jnp.float32)
    adjoint = (
        own_spectra * jnp.concatenate([power_sum, power_sum])[None, :]
        - jnp.concatenate([mix_real, mix_imag], axis=1)
    ) / stations
    adj_real, adj_imag = (adjoint[:, :local_freqs], adjoint[:, local_freqs:])
    green_bank = green.reshape(green.shape[0], 2 * local_freqs)
    green_ids = jnp.arange(green_bank.shape[0], dtype=jnp.int32)
    pick_hot = (green_index[:, :, None] == green_ids).astype(jnp.bfloat16)
    picked = jnp.einsum(
        "npg,gf->npf", pick_hot, green_bank, preferred_element_type=jnp.bfloat16
    ).astype(jnp.float32)
    pick_real, pick_imag = (picked[..., :local_freqs], picked[..., local_freqs:])
    weighted = jnp.concatenate(
        [
            adj_real[None] * pick_real + adj_imag[None] * pick_imag,
            adj_real[None] * pick_imag - adj_imag[None] * pick_real,
        ],
        axis=-1,
    ).astype(jnp.bfloat16)
    tiles_all = TILE_DEV * lax.axis_size("src")
    tile_hot = (tile_index[:, :, None] == jnp.arange(tiles_all, dtype=jnp.int32)).astype(
        jnp.bfloat16
    )
    tile_spectra = jnp.einsum(
        "npt,npf->tf", tile_hot, weighted, preferred_element_type=jnp.float32
    ) * math.sqrt(tiles_all / (stations * green_index.shape[0]))
    summed = lax.psum(tile_spectra, "blk")
    point_share = TP // lax.axis_size("blk")
    points = blk_index * point_share + jnp.arange(point_share, dtype=jnp.int32)
    tile_image = jnp.dot(
        summed, mode_table(freq_ids, points, TILE_SIDE), precision=lax.Precision.HIGHEST
    ) / math.sqrt(F)
    return lax.psum_scatter(tile_image, "src", scatter_dimension=0, tiled=True)

LANES = 128
BOTH = ("blk", "src")
HIGHEST = lax.Precision.HIGHEST
NT_DIMS = (((1,), (1,)), ((), ()))
TN_DIMS = (((0,), (0,)), ((), ()))
VMEM_BYTES = 20 * 1024 * 1024
PARTS_TYPE = jnp.bfloat16


def split_bf16(values):
    high = values.astype(jnp.bfloat16)
    low = (values - high.astype(np.float32)).astype(jnp.bfloat16)
    return high, low


def forward_tables(n_src, n_blk):
    steps = NT // LANES
    per_src = steps // n_src
    own = np.arange(n_src)
    order = np.stack(
        [np.concatenate([(s ^ k) * per_src + np.arange(per_src) for k in range(n_src)]) for s in own]
    )
    rows = np.arange(steps)
    angle = 2 * np.pi / steps * ((rows[None, :, None] * order[:, None, :]) % steps)
    first = np.concatenate([np.cos(angle), -np.sin(angle)], axis=1).astype(np.float32)
    first = np.concatenate(split_bf16(first), axis=1)
    lanes = np.arange(LANES)
    angle = 2 * np.pi / NT * ((lanes[:, None] * lanes[None, :]) % NT)
    twiddle = np.stack([np.cos(angle), -np.sin(angle)]).astype(np.float32)
    devices = np.arange(n_src * n_blk)
    block = devices % n_src * n_blk + devices // n_src
    angle = 2 * np.pi / steps * ((block[:, None] * lanes[None, :]) % steps)
    cos, sin = np.cos(angle), np.sin(angle)
    third = np.concatenate(
        [np.concatenate([cos, sin], axis=1), np.concatenate([-sin, cos], axis=1)], axis=0
    )
    third = split_bf16((third / math.sqrt(NT)).astype(np.float32))
    return first, twiddle, np.concatenate(third, axis=0)


def mode_tables(n_src, n_blk, scale):
    side = np.arange(TILE_SIDE)
    angle = 2 * np.pi / TILE_SIDE * ((side[:, None] * side[None, :]) % TILE_SIDE)
    cos, sin = np.cos(angle), np.sin(angle)
    low = np.zeros((2, 2, TILE_SIDE, 2, 2, TILE_SIDE))
    for parity in range(2):
        low[0, parity, :, parity, 0] = cos
        low[0, parity, :, parity, 1] = sin
        low[1, parity, :, parity, 0] = -sin
        low[1, parity, :, parity, 1] = cos
    low = low.reshape(4 * TILE_SIDE, 4 * TILE_SIDE) * scale
    devices = np.arange(n_src * n_blk)
    block = np.stack(
        [devices % n_src * n_blk + ((devices // n_src) ^ other) for other in range(2)], axis=1
    )
    high_freqs = block[..., None] * 2 + np.arange(2)
    angle = 2 * np.pi / TILE_SIDE * ((side[:, None, None, None] * high_freqs[None]) % TILE_SIDE)
    part = np.stack([np.cos(angle), -np.sin(angle)], axis=-1).reshape(
        n_blk, TILE_SIDE // n_blk, n_src * n_blk, 2, 4
    )
    high = np.zeros((n_blk, 2, TILE_SIDE // n_blk, n_src * n_blk, 2, 2, 4))
    for half in range(2):
        high[:, half, :, :, :, half] = part
    high = high.reshape(n_blk, 2 * TILE_SIDE // n_blk, 16 * n_src * n_blk)
    high = split_bf16((high / math.sqrt(F)).astype(np.float32))
    return low.astype(np.float32), np.concatenate(high, axis=1)


def spectra_kernel(n_src, *refs):
    pieces = refs[:n_src]
    first_ref, twiddle_ref, third_ref, out_ref, samples, reals, imags = refs[n_src:]
    stations, local = pieces[1].shape
    src_index = lax.axis_index("src")
    own = pieces[0].at[pl.ds(pl.multiple_of(src_index * stations, stations), stations), :]
    pieces = (own,) + pieces[1:]
    per_src = local // LANES
    steps = per_src * n_src
    count = third_ref.shape[0] // 4
    first = first_ref[src_index]
    for k in range(n_src):
        for a in range(per_src):
            samples[pl.ds(k * per_src + a, stations, stride=steps), :] = pieces[k][
                :, a * LANES : (a + 1) * LANES
            ].astype(jnp.float32)
    twiddle_real, twiddle_imag = twiddle_ref[0], twiddle_ref[1]
    third = third_ref[...]
    for station in range(0, stations, 2):
        rows = jnp.concatenate(
            [samples[(station + h) * steps : (station + h + 1) * steps, :] for h in range(2)], axis=1
        ).astype(jnp.bfloat16)
        parts = jnp.dot(first, rows, preferred_element_type=jnp.float32)
        reals_here = parts[:steps] + parts[2 * steps : 3 * steps]
        imags_here = parts[steps : 2 * steps] + parts[3 * steps :]
        turned = []
        for h in range(2):
            at = slice(h * LANES, (h + 1) * LANES)
            real = jnp.concatenate([reals_here[:, at]] * (LANES // steps), axis=0)
            imag = jnp.concatenate([imags_here[:, at]] * (LANES // steps), axis=0)
            turned.append(
                jnp.concatenate(
                    [
                        real * twiddle_real - imag * twiddle_imag,
                        real * twiddle_imag + imag * twiddle_real,
                    ],
                    axis=1,
                )
            )
        turned = jnp.concatenate(turned, axis=0)
        high = turned.astype(jnp.bfloat16)
        low = (turned - high.astype(jnp.float32)).astype(jnp.bfloat16)
        result = lax.dot_general(third, high, NT_DIMS, preferred_element_type=jnp.float32)
        result = (
            result[: 2 * count]
            + result[2 * count :]
            + lax.dot_general(
                third[: 2 * count], low, NT_DIMS, preferred_element_type=jnp.float32
            )
        )
        for h in range(2):
            at = slice(h * LANES, (h + 1) * LANES)
            reals[pl.ds(station + h, count, stride=stations), :] = result[:count, at]
            imags[pl.ds(station + h, count, stride=stations), :] = result[count:, at]
    out_ref[:, :LANES] = reals[...].astype(jnp.bfloat16)
    out_ref[:, LANES:] = imags[...].astype(jnp.bfloat16)


def adjoint_kernel(panels, slots, n_src, chunk, *refs):
    packs = refs[:panels]
    observed_ref, green_ref, spectra_ref, other_ref, low_ref, out_ref = refs[panels : panels + 6]
    spectra, classes, numbers, bank, green, mixed, total = refs[panels + 6 :]
    stations = spectra_ref.shape[0]
    panel = classes.shape[0] // panels
    class_count = bank.shape[0]
    tiles = total.shape[0]
    blk_index = lax.axis_index("blk")
    for other in range(2):
        at = pl.ds(pl.multiple_of((blk_index ^ other) * LANES, LANES), LANES)
        lanes = slice(2 * other * LANES, 2 * (other + 1) * LANES)
        pair = observed_ref[:, :, at].astype(jnp.float32)
        bank[:, lanes] = jnp.concatenate([pair[:, 0, :], pair[:, 1, :]], axis=1)
        pair = green_ref[:, :, at].astype(jnp.float32)
        pair = jnp.concatenate([pair[:, 0, :], pair[:, 1, :]], axis=1)
        green[:, lanes] = pair.astype(jnp.bfloat16)
    for k, pack in enumerate(packs):
        classes[k * panel : (k + 1) * panel, :] = pack[:panel].astype(jnp.float32)
        ids = pack[panel : panel + 16, :LANES].astype(jnp.int32)
        for row in range(2):
            numbers[k, row : row + 1] = jnp.concatenate(
                [ids[8 * row + slot : 8 * row + slot + 1, :panel] for slot in range(slots)], axis=1
            )
    spectra[:, : 2 * LANES] = spectra_ref[...]
    spectra[:, 2 * LANES :] = other_ref[...]
    widened = spectra[...].astype(jnp.float32)
    squares = jnp.sum(widened * widened, axis=0, keepdims=True)
    lanes = [slice(part * LANES, (part + 1) * LANES) for part in range(4)]
    power = []
    for real, imag in (lanes[:2], lanes[2:]):
        power += [squares[:, real] + squares[:, imag]] * 2
    power = jnp.concatenate(power, axis=1)
    green_ids = lax.broadcasted_iota(jnp.int32, (green.shape[0], slots * panel), 0)
    tile_ids = lax.broadcasted_iota(jnp.int32, (tiles, slots * panel), 0)
    class_ids = lax.broadcasted_iota(jnp.int32, (class_count, stations), 0).astype(jnp.float32)
    class_ids = class_ids.astype(jnp.bfloat16).reshape(1, class_count // 16, 16, stations)
    total[...] = jnp.zeros_like(total)

    def mix(place):
        start = pl.multiple_of(place * panel, panel)
        places = [pl.ds(start + part * chunk, chunk) for part in range(panel // chunk)]

        def one_hot(at):
            wide = jnp.broadcast_to(classes[at, :][:, None, :], (chunk, 16, stations))
            wide = wide.astype(jnp.bfloat16)[:, None]
            hot = jnp.where(wide == class_ids, jnp.bfloat16(1.0), jnp.bfloat16(0.0))
            return hot.reshape(chunk * class_count, stations)

        def reduce(at, grouped):
            grouped = grouped.reshape(chunk, class_count, 4 * LANES)
            for real, imag in (lanes[:2], lanes[2:]):
                obs_real, obs_imag = bank[:, real][None], bank[:, imag][None]
                group_real, group_imag = grouped[..., real], grouped[..., imag]
                mixed[at, real] = jnp.sum(obs_real * group_real - obs_imag * group_imag, axis=1)
                mixed[at, imag] = jnp.sum(obs_real * group_imag + obs_imag * group_real, axis=1)

        hot, before = one_hot(places[0]), None
        for part, at in enumerate(places):
            grouped = jnp.dot(hot, spectra[...], preferred_element_type=jnp.float32)
            if part + 1 < len(places):
                hot = one_hot(places[part + 1])
            if before is not None:
                reduce(*before)
            before = (at, grouped)
        reduce(*before)

    def gather(place):
        at = pl.ds(pl.multiple_of(place * panel, panel), panel)
        owner = blk_index ^ (2 * place)
        own = spectra[pl.ds(pl.multiple_of(owner * panel, panel), panel), :].astype(jnp.float32)
        adjoint = (own * power - mixed[at, :]) * (1.0 / stations)
        ids = numbers[place]
        pick = jnp.where(ids[:1] == green_ids, 1.0, 0.0).astype(jnp.bfloat16)
        tile = jnp.where(ids[1:2] == tile_ids, 1.0, 0.0).astype(jnp.bfloat16)
        all_picked = lax.dot_general(
            pick, green[...], TN_DIMS, preferred_element_type=jnp.float32
        )
        weighted = []
        for slot in range(slots):
            picked = all_picked[slot * panel : (slot + 1) * panel]
            row = []
            for real, imag in (lanes[:2], lanes[2:]):
                row.append(adjoint[:, real] * picked[:, real] + adjoint[:, imag] * picked[:, imag])
                row.append(adjoint[:, real] * picked[:, imag] - adjoint[:, imag] * picked[:, real])
            weighted.append(jnp.concatenate(row, axis=1).astype(jnp.bfloat16))
        total[...] += jnp.dot(
            tile,
            jnp.concatenate(weighted, axis=0),
            preferred_element_type=jnp.float32,
        )

    def mix_panel(place, carry):
        mix(place)
        return carry

    lax.fori_loop(0, panels, mix_panel, 0)
    for place in range(panels):
        gather(place)
    low = [
        jnp.dot(
            total[:, at], low_ref[...], precision=HIGHEST, preferred_element_type=jnp.float32
        )
        for at in (slice(0, 2 * LANES), slice(2 * LANES, 4 * LANES))
    ]
    rows = []
    for owner in range(n_src):
        for other in range(2):
            for half in range(2):
                at = owner * (tiles // n_src) + 2 * half
                for part in range(4):
                    side = slice(part * TILE_SIDE, (part + 1) * TILE_SIDE)
                    rows.append(
                        jnp.concatenate(
                            [low[other][at : at + 1, side], low[other][at + 1 : at + 2, side]], axis=1
                        )
                    )
    rows = jnp.concatenate(rows, axis=0).astype(out_ref.dtype)
    for copy in range(out_ref.shape[0] // rows.shape[0]):
        out_ref[copy * 16 * n_src : (copy + 1) * 16 * n_src, :] = rows


def image_kernel(high_ref, parts_ref, out_ref):
    high = high_ref[lax.axis_index("blk")]
    image = jnp.dot(high, parts_ref[...], preferred_element_type=jnp.float32)
    count = image.shape[0] // 2
    image = image[:count] + image[count:]
    rows = count // 2
    for tile in range(out_ref.shape[0]):
        half, side = tile // 2, tile % 2
        for row in range(rows):
            at = half * rows + row
            out_ref[tile : tile + 1, row * TILE_SIDE : (row + 1) * TILE_SIDE] = image[
                at : at + 1, side * TILE_SIDE : (side + 1) * TILE_SIDE
            ]


def swap(values, axis, distance):
    size = lax.axis_size(axis)
    return lax.ppermute(values, axis, [(i, i ^ distance) for i in range(size)])


def split_body(windows, observed, pair_class, green, green_index, tile_index):
    n_blk, n_src = lax.axis_size("blk"), lax.axis_size("src")
    src_index = lax.axis_index("src")
    panel, local = windows.shape
    stations = panel * n_blk
    slots = green_index.shape[0]
    tiles = TILE_DEV * n_src
    share = panel // n_src
    pieces = [
        lax.dynamic_slice_in_dim(windows, (src_index ^ k) * share, share, 0)
        for k in range(1, n_src)
    ]
    pieces = [windows] + [swap(piece, "src", k + 1) for k, piece in enumerate(pieces)]

    def widen(ids):
        return jnp.pad(ids, ((0, 8 - slots), (0, stations - panel)))

    pack = jnp.concatenate([pair_class, widen(green_index), widen(tile_index)], axis=0).astype(
        jnp.bfloat16
    )
    packs = [pack] + [swap(pack, "blk", k) for k in range(2, n_blk, 2)]

    first, twiddle, third = forward_tables(n_src, n_blk)
    low, high = mode_tables(n_src, n_blk, math.sqrt(tiles / (stations * slots)))
    devices = n_blk * n_src
    params = pltpu.CompilerParams(vmem_limit_bytes=VMEM_BYTES)
    blocks = pl.pallas_call(
        functools.partial(spectra_kernel, n_src),
        out_shape=jax.ShapeDtypeStruct((devices * share, 2 * LANES), jnp.bfloat16),
        scratch_shapes=[
            pltpu.VMEM((share * NT // LANES, LANES), jnp.float32),
            pltpu.VMEM((devices * share, LANES), jnp.float32),
            pltpu.VMEM((devices * share, LANES), jnp.float32),
        ],
        compiler_params=params,
        name="spectra",
    )(*pieces, first, twiddle, third)
    spectra = lax.all_to_all(
        blocks.reshape(devices, share, 2 * LANES), BOTH, 0, 0, tiled=True
    ).reshape(stations, 2 * LANES)
    class_count = observed.shape[0]
    panels = n_blk // 2
    spectra, packs = lax.optimization_barrier((spectra, packs))
    parts = pl.pallas_call(
        functools.partial(adjoint_kernel, panels, slots, n_src, 16),
        out_shape=jax.ShapeDtypeStruct((16 * devices, 2 * TILE_SIDE), PARTS_TYPE),
        scratch_shapes=[
            pltpu.VMEM((stations, 4 * LANES), jnp.bfloat16),
            pltpu.VMEM((panels * panel, stations), jnp.float32),
            pltpu.VMEM((panels, 8, slots * panel), jnp.int32),
            pltpu.VMEM((class_count, 4 * LANES), jnp.float32),
            pltpu.VMEM((green.shape[0], 4 * LANES), jnp.bfloat16),
            pltpu.VMEM((panels * panel, 4 * LANES), jnp.float32),
            pltpu.VMEM((tiles, 4 * LANES), jnp.float32),
        ],
        compiler_params=params,
        name="adjoint",
    )(*packs, observed, green, spectra, swap(spectra, "blk", 1), low)
    parts = lax.all_to_all(
        parts.reshape(devices, 16, 2 * TILE_SIDE), BOTH, 0, 0, tiled=True
    ).reshape(16 * devices, 2 * TILE_SIDE)
    return pl.pallas_call(
        image_kernel,
        out_shape=jax.ShapeDtypeStruct((TILE_DEV, TP // n_blk), jnp.float32),
        compiler_params=params,
        name="image",
    )(high, parts)


def solution(mesh):
    in_specs = (
        P("blk", "src"),
        P(None, None, "src"),
        P("blk", None),
        P(None, None, "src"),
        P(None, "blk"),
        P(None, "blk"),
    )
    out_specs = P("src", "blk")
    whole_lanes = mesh.size * LANES == F
    body = split_body if whole_lanes else general_body
    return jax.shard_map(body, mesh=mesh, in_specs=in_specs, out_specs=out_specs, check_vma=False)
```

```python
import functools
import math

import jax
import jax.numpy as jnp
import numpy as np
from jax import lax
from jax.experimental import pallas as pl
from jax.experimental.pallas import tpu as pltpu
from jax.sharding import PartitionSpec as P

NT = 8192
TILE_SIDE = 64
TILE_DEV = 4
F = 4096
TP = 4096


def trig_pair(phase_index, period):
    angle_rad = phase_index.astype(jnp.float32) * (2.0 * math.pi / period)
    return (jnp.cos(angle_rad), jnp.sin(angle_rad))


def dft_rows(count, freq_ids, period):
    amp_scale = 1.0 / math.sqrt(period)
    local_freqs = freq_ids.shape[0]
    high_ids = jnp.arange(count // 128, dtype=jnp.int32)
    low_ids = jnp.arange(128, dtype=jnp.int32)
    high_cos, high_sin = trig_pair(high_ids[:, None] * 128 * freq_ids[None, :] % period, period)
    low_cos, low_sin = trig_pair(low_ids[:, None] * freq_ids[None, :] % period, period)
    cos_part = (
        high_cos[:, None, :] * low_cos[None] - high_sin[:, None, :] * low_sin[None]
    ).reshape(count, local_freqs)
    sin_part = (
        high_sin[:, None, :] * low_cos[None] + high_cos[:, None, :] * low_sin[None]
    ).reshape(count, local_freqs)
    return jnp.concatenate([cos_part * amp_scale, -sin_part * amp_scale], axis=1).astype(
        jnp.bfloat16
    )


def mode_table(freq_ids, points, edge_cells):
    phase_index = freq_ids[:, None] % edge_cells * (points[None, :] % edge_cells) + freq_ids[
        :, None
    ] // edge_cells * (points[None, :] // edge_cells)
    angle_rad = (phase_index % edge_cells).astype(jnp.float32) * (2.0 * math.pi / edge_cells)
    return jnp.concatenate([jnp.cos(angle_rad), -jnp.sin(angle_rad)], axis=0)


def general_body(windows, observed, pair_class, green, green_index, tile_index):
    panel_rows = windows.shape[0]
    local_freqs = observed.shape[2]
    class_count = observed.shape[0]
    src_index = lax.axis_index("src")
    blk_index = lax.axis_index("blk")
    stations = panel_rows * lax.axis_size("blk")
    freq_ids = src_index * local_freqs + jnp.arange(local_freqs, dtype=jnp.int32)
    shard_piece = lax.all_gather(windows, "src", axis=1, tiled=True)
    table_rows = dft_rows(shard_piece.shape[1], freq_ids, NT)
    spectra = jnp.dot(shard_piece, table_rows, preferred_element_type=jnp.float32).astype(
        jnp.bfloat16
    )
    class_ids = jnp.arange(class_count, dtype=jnp.int32)
    shard_piece = lax.all_gather(spectra, "blk", axis=0, tiled=True)
    widened = shard_piece.astype(jnp.float32)
    far_real = widened[:, :local_freqs]
    far_imag = widened[:, local_freqs:]
    power_sum = jnp.sum(far_real * far_real + far_imag * far_imag, axis=0)
    class_hot = (pair_class[:, :, None] == class_ids).astype(jnp.bfloat16)
    grouped = jnp.einsum("ijk,jf->ikf", class_hot, shard_piece, preferred_element_type=jnp.float32)
    power_sum, grouped = (power_sum, grouped)
    obs_table = observed.reshape(class_count, 2 * local_freqs).astype(jnp.float32)
    obs_real, obs_imag = (obs_table[:, :local_freqs], obs_table[:, local_freqs:])
    group_real, group_imag = (grouped[..., :local_freqs], grouped[..., local_freqs:])
    highest = lax.Precision.HIGHEST
    mix_real = jnp.einsum("kf,ikf->if", obs_real, group_real, precision=highest) - jnp.einsum(
        "kf,ikf->if", obs_imag, group_imag, precision=highest
    )
    mix_imag = jnp.einsum("kf,ikf->if", obs_real, group_imag, precision=highest) + jnp.einsum(
        "kf,ikf->if", obs_imag, group_real, precision=highest
    )
    own_spectra = spectra.astype(jnp.float32)
    adjoint = (
        own_spectra * jnp.concatenate([power_sum, power_sum])[None, :]
        - jnp.concatenate([mix_real, mix_imag], axis=1)
    ) / stations
    adj_real, adj_imag = (adjoint[:, :local_freqs], adjoint[:, local_freqs:])
    green_bank = green.reshape(green.shape[0], 2 * local_freqs)
    green_ids = jnp.arange(green_bank.shape[0], dtype=jnp.int32)
    pick_hot = (green_index[:, :, None] == green_ids).astype(jnp.bfloat16)
    picked = jnp.einsum(
        "npg,gf->npf", pick_hot, green_bank, preferred_element_type=jnp.bfloat16
    ).astype(jnp.float32)
    pick_real, pick_imag = (picked[..., :local_freqs], picked[..., local_freqs:])
    weighted = jnp.concatenate(
        [
            adj_real[None] * pick_real + adj_imag[None] * pick_imag,
            adj_real[None] * pick_imag - adj_imag[None] * pick_real,
        ],
        axis=-1,
    ).astype(jnp.bfloat16)
    tiles_all = TILE_DEV * lax.axis_size("src")
    tile_hot = (tile_index[:, :, None] == jnp.arange(tiles_all, dtype=jnp.int32)).astype(
        jnp.bfloat16
    )
    tile_spectra = jnp.einsum(
        "npt,npf->tf", tile_hot, weighted, preferred_element_type=jnp.float32
    ) * math.sqrt(tiles_all / (stations * green_index.shape[0]))
    summed = lax.psum(tile_spectra, "blk")
    point_share = TP // lax.axis_size("blk")
    points = blk_index * point_share + jnp.arange(point_share, dtype=jnp.int32)
    tile_image = jnp.dot(
        summed, mode_table(freq_ids, points, TILE_SIDE), precision=lax.Precision.HIGHEST
    ) / math.sqrt(F)
    return lax.psum_scatter(tile_image, "src", scatter_dimension=0, tiled=True)

LANES = 128
BOTH = ("blk", "src")
HIGHEST = lax.Precision.HIGHEST
NT_DIMS = (((1,), (1,)), ((), ()))
TN_DIMS = (((0,), (0,)), ((), ()))
VMEM_BYTES = 20 * 1024 * 1024
PARTS_TYPE = jnp.bfloat16


def split_bf16(values):
    high = values.astype(jnp.bfloat16)
    low = (values - high.astype(np.float32)).astype(jnp.bfloat16)
    return high, low


def forward_tables(n_src, n_blk):
    steps = NT // LANES
    rows = np.arange(steps)
    angle = 2 * np.pi / steps * ((rows[:, None] * rows[None, :]) % steps)
    first = np.concatenate([np.cos(angle), -np.sin(angle)], axis=0).astype(np.float32)
    first = np.concatenate(split_bf16(first), axis=0)
    lanes = np.arange(LANES)
    angle = 2 * np.pi / NT * ((lanes[:, None] * lanes[None, :]) % NT)
    twiddle = np.stack([np.cos(angle), -np.sin(angle)]).astype(np.float32)
    devices = np.arange(n_src * n_blk)
    block = devices % n_src * n_blk + devices // n_src
    angle = 2 * np.pi / steps * ((block[:, None] * lanes[None, :]) % steps)
    cos, sin = np.cos(angle), np.sin(angle)
    third = np.concatenate(
        [np.concatenate([cos, sin], axis=1), np.concatenate([-sin, cos], axis=1)], axis=0
    )
    third = split_bf16((third / math.sqrt(NT)).astype(np.float32))
    return first, twiddle, np.concatenate(third, axis=0)


def mode_tables(n_src, n_blk, scale):
    side = np.arange(TILE_SIDE)
    angle = 2 * np.pi / TILE_SIDE * ((side[:, None] * side[None, :]) % TILE_SIDE)
    cos, sin = np.cos(angle), np.sin(angle)
    low = np.zeros((2, 2, TILE_SIDE, 2, 2, TILE_SIDE))
    for parity in range(2):
        low[0, parity, :, parity, 0] = cos
        low[0, parity, :, parity, 1] = sin
        low[1, parity, :, parity, 0] = -sin
        low[1, parity, :, parity, 1] = cos
    low = low.reshape(4 * TILE_SIDE, 4 * TILE_SIDE) * scale
    devices = np.arange(n_src * n_blk)
    block = np.stack(
        [devices % n_src * n_blk + ((devices // n_src) ^ other) for other in range(2)], axis=1
    )
    high_freqs = block[..., None] * 2 + np.arange(2)
    angle = 2 * np.pi / TILE_SIDE * ((side[:, None, None, None] * high_freqs[None]) % TILE_SIDE)
    part = np.stack([np.cos(angle), -np.sin(angle)], axis=-1).reshape(
        n_blk, TILE_SIDE // n_blk, n_src * n_blk, 2, 4
    )
    high = np.zeros((n_blk, 2, TILE_SIDE // n_blk, n_src * n_blk, 2, 2, 4))
    for half in range(2):
        high[:, half, :, :, :, half] = part
    high = high.reshape(n_blk, 2 * TILE_SIDE // n_blk, 16 * n_src * n_blk)
    high = split_bf16((high / math.sqrt(F)).astype(np.float32))
    return low.astype(np.float32), np.concatenate(high, axis=1)


def spectra_kernel(n_src, *refs):
    pieces = refs[:n_src]
    first_ref, twiddle_ref, third_ref, out_ref, samples, reals, imags = refs[n_src:]
    stations, local = pieces[1].shape
    src_index = lax.axis_index("src")
    per_src = local // LANES
    steps = per_src * n_src
    count = third_ref.shape[0] // 4
    first = first_ref[...]
    for k in range(n_src):
        start = (src_index ^ k) * per_src
        for a in range(per_src):
            samples[pl.ds(start + a, stations, stride=steps), :] = pieces[k][
                :, a * LANES : (a + 1) * LANES
            ].astype(jnp.float32)
    twiddle_real, twiddle_imag = twiddle_ref[0], twiddle_ref[1]
    third = third_ref[...]
    for station in range(0, stations, 2):
        rows = jnp.concatenate(
            [samples[(station + h) * steps : (station + h + 1) * steps, :] for h in range(2)], axis=1
        ).astype(jnp.bfloat16)
        parts = jnp.dot(first, rows, preferred_element_type=jnp.float32)
        reals_here = parts[:steps] + parts[2 * steps : 3 * steps]
        imags_here = parts[steps : 2 * steps] + parts[3 * steps :]
        turned = []
        for h in range(2):
            at = slice(h * LANES, (h + 1) * LANES)
            real = jnp.concatenate([reals_here[:, at]] * (LANES // steps), axis=0)
            imag = jnp.concatenate([imags_here[:, at]] * (LANES // steps), axis=0)
            turned.append(
                jnp.concatenate(
                    [
                        real * twiddle_real - imag * twiddle_imag,
                        real * twiddle_imag + imag * twiddle_real,
                    ],
                    axis=1,
                )
            )
        turned = jnp.concatenate(turned, axis=0)
        high = turned.astype(jnp.bfloat16)
        low = (turned - high.astype(jnp.float32)).astype(jnp.bfloat16)
        result = lax.dot_general(third, high, NT_DIMS, preferred_element_type=jnp.float32)
        result = (
            result[: 2 * count]
            + result[2 * count :]
            + lax.dot_general(
                third[: 2 * count], low, NT_DIMS, preferred_element_type=jnp.float32
            )
        )
        for h in range(2):
            at = slice(h * LANES, (h + 1) * LANES)
            reals[pl.ds(station + h, count, stride=stations), :] = result[:count, at]
            imags[pl.ds(station + h, count, stride=stations), :] = result[count:, at]
    out_ref[:, :LANES] = reals[...].astype(jnp.bfloat16)
    out_ref[:, LANES:] = imags[...].astype(jnp.bfloat16)


def adjoint_kernel(panels, slots, n_src, chunk, *refs):
    packs = refs[:panels]
    observed_ref, green_ref, spectra_ref, other_ref, low_ref, out_ref = refs[panels : panels + 6]
    spectra, classes, numbers, bank, green, mixed, total = refs[panels + 6 :]
    stations = spectra_ref.shape[0]
    panel = classes.shape[0] // panels
    class_count = bank.shape[0]
    tiles = total.shape[0]
    blk_index = lax.axis_index("blk")
    for other in range(2):
        at = pl.ds(pl.multiple_of((blk_index ^ other) * LANES, LANES), LANES)
        lanes = slice(2 * other * LANES, 2 * (other + 1) * LANES)
        pair = observed_ref[:, :, at].astype(jnp.float32)
        bank[:, lanes] = jnp.concatenate([pair[:, 0, :], pair[:, 1, :]], axis=1)
        pair = green_ref[:, :, at].astype(jnp.float32)
        pair = jnp.concatenate([pair[:, 0, :], pair[:, 1, :]], axis=1)
        green[:, lanes] = pair.astype(jnp.bfloat16)
    for k, pack in enumerate(packs):
        classes[k * panel : (k + 1) * panel, :] = pack[:panel].astype(jnp.float32)
        ids = pack[panel : panel + 16, :LANES].astype(jnp.int32)
        for row in range(2):
            numbers[k, row : row + 1] = jnp.concatenate(
                [ids[8 * row + slot : 8 * row + slot + 1, :panel] for slot in range(slots)], axis=1
            )
    spectra[:, : 2 * LANES] = spectra_ref[...]
    spectra[:, 2 * LANES :] = other_ref[...]
    widened = spectra[...].astype(jnp.float32)
    squares = jnp.sum(widened * widened, axis=0, keepdims=True)
    lanes = [slice(part * LANES, (part + 1) * LANES) for part in range(4)]
    power = []
    for real, imag in (lanes[:2], lanes[2:]):
        power += [squares[:, real] + squares[:, imag]] * 2
    power = jnp.concatenate(power, axis=1)
    green_ids = lax.broadcasted_iota(jnp.int32, (green.shape[0], slots * panel), 0)
    tile_ids = lax.broadcasted_iota(jnp.int32, (tiles, slots * panel), 0)
    class_ids = lax.broadcasted_iota(jnp.int32, (class_count, stations), 0).astype(jnp.float32)
    class_ids = class_ids.astype(jnp.bfloat16).reshape(1, class_count // 16, 16, stations)
    total[...] = jnp.zeros_like(total)

    def mix(place):
        start = pl.multiple_of(place * panel, panel)
        places = [pl.ds(start + part * chunk, chunk) for part in range(panel // chunk)]

        def one_hot(at):
            wide = jnp.broadcast_to(classes[at, :][:, None, :], (chunk, 16, stations))
            wide = wide.astype(jnp.bfloat16)[:, None]
            hot = jnp.where(wide == class_ids, jnp.bfloat16(1.0), jnp.bfloat16(0.0))
            return hot.reshape(chunk * class_count, stations)

        def reduce(at, grouped):
            grouped = grouped.reshape(chunk, class_count, 4 * LANES)
            for real, imag in (lanes[:2], lanes[2:]):
                obs_real, obs_imag = bank[:, real][None], bank[:, imag][None]
                group_real, group_imag = grouped[..., real], grouped[..., imag]
                mixed[at, real] = jnp.sum(obs_real * group_real - obs_imag * group_imag, axis=1)
                mixed[at, imag] = jnp.sum(obs_real * group_imag + obs_imag * group_real, axis=1)

        hot, before = one_hot(places[0]), None
        for part, at in enumerate(places):
            grouped = jnp.dot(hot, spectra[...], preferred_element_type=jnp.float32)
            if part + 1 < len(places):
                hot = one_hot(places[part + 1])
            if before is not None:
                reduce(*before)
            before = (at, grouped)
        reduce(*before)

    def gather(place):
        at = pl.ds(pl.multiple_of(place * panel, panel), panel)
        owner = blk_index ^ (2 * place)
        own = spectra[pl.ds(pl.multiple_of(owner * panel, panel), panel), :].astype(jnp.float32)
        adjoint = (own * power - mixed[at, :]) * (1.0 / stations)
        ids = numbers[place]
        pick = jnp.where(ids[:1] == green_ids, 1.0, 0.0).astype(jnp.bfloat16)
        tile = jnp.where(ids[1:2] == tile_ids, 1.0, 0.0).astype(jnp.bfloat16)
        all_picked = lax.dot_general(
            pick, green[...], TN_DIMS, preferred_element_type=jnp.float32
        )
        weighted = []
        for slot in range(slots):
            picked = all_picked[slot * panel : (slot + 1) * panel]
            row = []
            for real, imag in (lanes[:2], lanes[2:]):
                row.append(adjoint[:, real] * picked[:, real] + adjoint[:, imag] * picked[:, imag])
                row.append(adjoint[:, real] * picked[:, imag] - adjoint[:, imag] * picked[:, real])
            weighted.append(jnp.concatenate(row, axis=1).astype(jnp.bfloat16))
        total[...] += jnp.dot(
            tile,
            jnp.concatenate(weighted, axis=0),
            preferred_element_type=jnp.float32,
        )

    mix(0)
    for place in range(1, panels):
        mix(place)
        gather(place - 1)
    gather(panels - 1)
    low = [
        jnp.dot(
            total[:, at], low_ref[...], precision=HIGHEST, preferred_element_type=jnp.float32
        )
        for at in (slice(0, 2 * LANES), slice(2 * LANES, 4 * LANES))
    ]
    rows = []
    for owner in range(n_src):
        for other in range(2):
            for half in range(2):
                at = owner * (tiles // n_src) + 2 * half
                for part in range(4):
                    side = slice(part * TILE_SIDE, (part + 1) * TILE_SIDE)
                    rows.append(
                        jnp.concatenate(
                            [low[other][at : at + 1, side], low[other][at + 1 : at + 2, side]], axis=1
                        )
                    )
    rows = jnp.concatenate(rows, axis=0).astype(out_ref.dtype)
    for copy in range(out_ref.shape[0] // rows.shape[0]):
        out_ref[copy * 16 * n_src : (copy + 1) * 16 * n_src, :] = rows


def image_kernel(high_ref, parts_ref, out_ref):
    high = high_ref[lax.axis_index("blk")]
    image = jnp.dot(high, parts_ref[...], preferred_element_type=jnp.float32)
    count = image.shape[0] // 2
    image = image[:count] + image[count:]
    rows = count // 2
    for tile in range(out_ref.shape[0]):
        half, side = tile // 2, tile % 2
        for row in range(rows):
            at = half * rows + row
            out_ref[tile : tile + 1, row * TILE_SIDE : (row + 1) * TILE_SIDE] = image[
                at : at + 1, side * TILE_SIDE : (side + 1) * TILE_SIDE
            ]


def swap(values, axis, distance):
    size = lax.axis_size(axis)
    return lax.ppermute(values, axis, [(i, i ^ distance) for i in range(size)])


def split_body(windows, observed, pair_class, green, green_index, tile_index):
    n_blk, n_src = lax.axis_size("blk"), lax.axis_size("src")
    src_index = lax.axis_index("src")
    panel, local = windows.shape
    stations = panel * n_blk
    slots = green_index.shape[0]
    tiles = TILE_DEV * n_src
    share = panel // n_src
    pieces = [
        lax.dynamic_slice_in_dim(windows, (src_index ^ k) * share, share, 0)
        for k in range(n_src)
    ]
    pieces = pieces[:1] + [swap(pieces[k], "src", k) for k in range(1, n_src)]

    def widen(ids):
        return jnp.pad(ids, ((0, 8 - slots), (0, stations - panel)))

    pack = jnp.concatenate([pair_class, widen(green_index), widen(tile_index)], axis=0).astype(
        jnp.bfloat16
    )
    packs = [pack] + [swap(pack, "blk", k) for k in range(2, n_blk, 2)]

    first, twiddle, third = forward_tables(n_src, n_blk)
    low, high = mode_tables(n_src, n_blk, math.sqrt(tiles / (stations * slots)))
    devices = n_blk * n_src
    params = pltpu.CompilerParams(vmem_limit_bytes=VMEM_BYTES)
    blocks = pl.pallas_call(
        functools.partial(spectra_kernel, n_src),
        out_shape=jax.ShapeDtypeStruct((devices * share, 2 * LANES), jnp.bfloat16),
        scratch_shapes=[
            pltpu.VMEM((share * NT // LANES, LANES), jnp.float32),
            pltpu.VMEM((devices * share, LANES), jnp.float32),
            pltpu.VMEM((devices * share, LANES), jnp.float32),
        ],
        compiler_params=params,
        name="spectra",
    )(*pieces, first, twiddle, third)
    spectra = lax.all_to_all(
        blocks.reshape(devices, share, 2 * LANES), BOTH, 0, 0, tiled=True
    ).reshape(stations, 2 * LANES)
    class_count = observed.shape[0]
    panels = n_blk // 2
    spectra, packs = lax.optimization_barrier((spectra, packs))
    parts = pl.pallas_call(
        functools.partial(adjoint_kernel, panels, slots, n_src, 16),
        out_shape=jax.ShapeDtypeStruct((16 * devices, 2 * TILE_SIDE), PARTS_TYPE),
        scratch_shapes=[
            pltpu.VMEM((stations, 4 * LANES), jnp.bfloat16),
            pltpu.VMEM((panels * panel, stations), jnp.float32),
            pltpu.VMEM((panels, 8, slots * panel), jnp.int32),
            pltpu.VMEM((class_count, 4 * LANES), jnp.float32),
            pltpu.VMEM((green.shape[0], 4 * LANES), jnp.bfloat16),
            pltpu.VMEM((panels * panel, 4 * LANES), jnp.float32),
            pltpu.VMEM((tiles, 4 * LANES), jnp.float32),
        ],
        compiler_params=params,
        name="adjoint",
    )(*packs, observed, green, spectra, swap(spectra, "blk", 1), low)
    parts = lax.all_to_all(
        parts.reshape(devices, 16, 2 * TILE_SIDE), BOTH, 0, 0, tiled=True
    ).reshape(16 * devices, 2 * TILE_SIDE)
    return pl.pallas_call(
        image_kernel,
        out_shape=jax.ShapeDtypeStruct((TILE_DEV, TP // n_blk), jnp.float32),
        compiler_params=params,
        name="image",
    )(high, parts)


def solution(mesh):
    in_specs = (
        P("blk", "src"),
        P(None, None, "src"),
        P("blk", None),
        P(None, None, "src"),
        P(None, "blk"),
        P(None, "blk"),
    )
    out_specs = P("src", "blk")
    whole_lanes = mesh.size * LANES == F
    body = split_body if whole_lanes else general_body
    return jax.shard_map(body, mesh=mesh, in_specs=in_specs, out_specs=out_specs, check_vma=False)
```

```python
import functools
import math

import jax
import jax.numpy as jnp
import numpy as np
from jax import lax
from jax.experimental import pallas as pl
from jax.experimental.pallas import tpu as pltpu
from jax.sharding import PartitionSpec as P

NT = 8192
TILE_SIDE = 64
TILE_DEV = 4
F = 4096
TP = 4096


def trig_pair(phase_index, period):
    angle_rad = phase_index.astype(jnp.float32) * (2.0 * math.pi / period)
    return (jnp.cos(angle_rad), jnp.sin(angle_rad))


def dft_rows(count, freq_ids, period):
    amp_scale = 1.0 / math.sqrt(period)
    local_freqs = freq_ids.shape[0]
    high_ids = jnp.arange(count // 128, dtype=jnp.int32)
    low_ids = jnp.arange(128, dtype=jnp.int32)
    high_cos, high_sin = trig_pair(high_ids[:, None] * 128 * freq_ids[None, :] % period, period)
    low_cos, low_sin = trig_pair(low_ids[:, None] * freq_ids[None, :] % period, period)
    cos_part = (
        high_cos[:, None, :] * low_cos[None] - high_sin[:, None, :] * low_sin[None]
    ).reshape(count, local_freqs)
    sin_part = (
        high_sin[:, None, :] * low_cos[None] + high_cos[:, None, :] * low_sin[None]
    ).reshape(count, local_freqs)
    return jnp.concatenate([cos_part * amp_scale, -sin_part * amp_scale], axis=1).astype(
        jnp.bfloat16
    )


def mode_table(freq_ids, points, edge_cells):
    phase_index = freq_ids[:, None] % edge_cells * (points[None, :] % edge_cells) + freq_ids[
        :, None
    ] // edge_cells * (points[None, :] // edge_cells)
    angle_rad = (phase_index % edge_cells).astype(jnp.float32) * (2.0 * math.pi / edge_cells)
    return jnp.concatenate([jnp.cos(angle_rad), -jnp.sin(angle_rad)], axis=0)


def general_body(windows, observed, pair_class, green, green_index, tile_index):
    panel_rows = windows.shape[0]
    local_freqs = observed.shape[2]
    class_count = observed.shape[0]
    src_index = lax.axis_index("src")
    blk_index = lax.axis_index("blk")
    stations = panel_rows * lax.axis_size("blk")
    freq_ids = src_index * local_freqs + jnp.arange(local_freqs, dtype=jnp.int32)
    shard_piece = lax.all_gather(windows, "src", axis=1, tiled=True)
    table_rows = dft_rows(shard_piece.shape[1], freq_ids, NT)
    spectra = jnp.dot(shard_piece, table_rows, preferred_element_type=jnp.float32).astype(
        jnp.bfloat16
    )
    class_ids = jnp.arange(class_count, dtype=jnp.int32)
    shard_piece = lax.all_gather(spectra, "blk", axis=0, tiled=True)
    widened = shard_piece.astype(jnp.float32)
    far_real = widened[:, :local_freqs]
    far_imag = widened[:, local_freqs:]
    power_sum = jnp.sum(far_real * far_real + far_imag * far_imag, axis=0)
    class_hot = (pair_class[:, :, None] == class_ids).astype(jnp.bfloat16)
    grouped = jnp.einsum("ijk,jf->ikf", class_hot, shard_piece, preferred_element_type=jnp.float32)
    power_sum, grouped = (power_sum, grouped)
    obs_table = observed.reshape(class_count, 2 * local_freqs).astype(jnp.float32)
    obs_real, obs_imag = (obs_table[:, :local_freqs], obs_table[:, local_freqs:])
    group_real, group_imag = (grouped[..., :local_freqs], grouped[..., local_freqs:])
    highest = lax.Precision.HIGHEST
    mix_real = jnp.einsum("kf,ikf->if", obs_real, group_real, precision=highest) - jnp.einsum(
        "kf,ikf->if", obs_imag, group_imag, precision=highest
    )
    mix_imag = jnp.einsum("kf,ikf->if", obs_real, group_imag, precision=highest) + jnp.einsum(
        "kf,ikf->if", obs_imag, group_real, precision=highest
    )
    own_spectra = spectra.astype(jnp.float32)
    adjoint = (
        own_spectra * jnp.concatenate([power_sum, power_sum])[None, :]
        - jnp.concatenate([mix_real, mix_imag], axis=1)
    ) / stations
    adj_real, adj_imag = (adjoint[:, :local_freqs], adjoint[:, local_freqs:])
    green_bank = green.reshape(green.shape[0], 2 * local_freqs)
    green_ids = jnp.arange(green_bank.shape[0], dtype=jnp.int32)
    pick_hot = (green_index[:, :, None] == green_ids).astype(jnp.bfloat16)
    picked = jnp.einsum(
        "npg,gf->npf", pick_hot, green_bank, preferred_element_type=jnp.bfloat16
    ).astype(jnp.float32)
    pick_real, pick_imag = (picked[..., :local_freqs], picked[..., local_freqs:])
    weighted = jnp.concatenate(
        [
            adj_real[None] * pick_real + adj_imag[None] * pick_imag,
            adj_real[None] * pick_imag - adj_imag[None] * pick_real,
        ],
        axis=-1,
    ).astype(jnp.bfloat16)
    tiles_all = TILE_DEV * lax.axis_size("src")
    tile_hot = (tile_index[:, :, None] == jnp.arange(tiles_all, dtype=jnp.int32)).astype(
        jnp.bfloat16
    )
    tile_spectra = jnp.einsum(
        "npt,npf->tf", tile_hot, weighted, preferred_element_type=jnp.float32
    ) * math.sqrt(tiles_all / (stations * green_index.shape[0]))
    summed = lax.psum(tile_spectra, "blk")
    point_share = TP // lax.axis_size("blk")
    points = blk_index * point_share + jnp.arange(point_share, dtype=jnp.int32)
    tile_image = jnp.dot(
        summed, mode_table(freq_ids, points, TILE_SIDE), precision=lax.Precision.HIGHEST
    ) / math.sqrt(F)
    return lax.psum_scatter(tile_image, "src", scatter_dimension=0, tiled=True)

LANES = 128
BOTH = ("blk", "src")
HIGHEST = lax.Precision.HIGHEST
NT_DIMS = (((1,), (1,)), ((), ()))
TN_DIMS = (((0,), (0,)), ((), ()))
VMEM_BYTES = 20 * 1024 * 1024
PARTS_TYPE = jnp.bfloat16


def split_bf16(values):
    high = values.astype(jnp.bfloat16)
    low = (values - high.astype(np.float32)).astype(jnp.bfloat16)
    return high, low


def forward_tables(n_src, n_blk):
    steps = NT // LANES
    rows = np.arange(steps)
    angle = 2 * np.pi / steps * ((rows[:, None] * rows[None, :]) % steps)
    first = np.concatenate([np.cos(angle), -np.sin(angle)], axis=0).astype(np.float32)
    first = np.concatenate(split_bf16(first), axis=0)
    lanes = np.arange(LANES)
    angle = 2 * np.pi / NT * ((lanes[:, None] * lanes[None, :]) % NT)
    twiddle = np.stack([np.cos(angle), -np.sin(angle)]).astype(np.float32)
    devices = np.arange(n_src * n_blk)
    block = devices % n_src * n_blk + devices // n_src
    angle = 2 * np.pi / steps * ((block[:, None] * lanes[None, :]) % steps)
    cos, sin = np.cos(angle), np.sin(angle)
    third = np.concatenate(
        [np.concatenate([cos, sin], axis=1), np.concatenate([-sin, cos], axis=1)], axis=0
    )
    third = split_bf16((third / math.sqrt(NT)).astype(np.float32))
    return first, twiddle, np.concatenate(third, axis=0)


def mode_tables(n_src, n_blk, scale):
    side = np.arange(TILE_SIDE)
    angle = 2 * np.pi / TILE_SIDE * ((side[:, None] * side[None, :]) % TILE_SIDE)
    cos, sin = np.cos(angle), np.sin(angle)
    low = np.zeros((2, 2, TILE_SIDE, 2, 2, TILE_SIDE))
    for parity in range(2):
        low[0, parity, :, parity, 0] = cos
        low[0, parity, :, parity, 1] = sin
        low[1, parity, :, parity, 0] = -sin
        low[1, parity, :, parity, 1] = cos
    low = low.reshape(4 * TILE_SIDE, 4 * TILE_SIDE) * scale
    devices = np.arange(n_src * n_blk)
    block = np.stack(
        [devices % n_src * n_blk + ((devices // n_src) ^ other) for other in range(2)], axis=1
    )
    high_freqs = block[..., None] * 2 + np.arange(2)
    angle = 2 * np.pi / TILE_SIDE * ((side[:, None, None, None] * high_freqs[None]) % TILE_SIDE)
    part = np.stack([np.cos(angle), -np.sin(angle)], axis=-1).reshape(
        n_blk, TILE_SIDE // n_blk, n_src * n_blk, 2, 4
    )
    high = np.zeros((n_blk, 2, TILE_SIDE // n_blk, n_src * n_blk, 2, 2, 4))
    for half in range(2):
        high[:, half, :, :, :, half] = part
    high = high.reshape(n_blk, 2 * TILE_SIDE // n_blk, 16 * n_src * n_blk)
    high = split_bf16((high / math.sqrt(F)).astype(np.float32))
    return low.astype(np.float32), np.concatenate(high, axis=1)


def spectra_kernel(n_src, *refs):
    pieces = refs[:n_src]
    first_ref, twiddle_ref, third_ref, out_ref, samples, reals, imags = refs[n_src:]
    stations, local = pieces[1].shape
    src_index = lax.axis_index("src")
    per_src = local // LANES
    steps = per_src * n_src
    count = third_ref.shape[0] // 4
    first = first_ref[...]
    for k in range(n_src):
        start = (src_index ^ k) * per_src
        for a in range(per_src):
            samples[pl.ds(start + a, stations, stride=steps), :] = pieces[k][
                :, a * LANES : (a + 1) * LANES
            ].astype(jnp.float32)
    twiddle_real, twiddle_imag = twiddle_ref[0], twiddle_ref[1]
    third = third_ref[...]
    for station in range(0, stations, 2):
        rows = jnp.concatenate(
            [samples[(station + h) * steps : (station + h + 1) * steps, :] for h in range(2)], axis=1
        ).astype(jnp.bfloat16)
        parts = jnp.dot(first, rows, preferred_element_type=jnp.float32)
        reals_here = parts[:steps] + parts[2 * steps : 3 * steps]
        imags_here = parts[steps : 2 * steps] + parts[3 * steps :]
        turned = []
        for h in range(2):
            at = slice(h * LANES, (h + 1) * LANES)
            real = jnp.concatenate([reals_here[:, at]] * (LANES // steps), axis=0)
            imag = jnp.concatenate([imags_here[:, at]] * (LANES // steps), axis=0)
            turned.append(
                jnp.concatenate(
                    [
                        real * twiddle_real - imag * twiddle_imag,
                        real * twiddle_imag + imag * twiddle_real,
                    ],
                    axis=1,
                )
            )
        turned = jnp.concatenate(turned, axis=0)
        high = turned.astype(jnp.bfloat16)
        low = (turned - high.astype(jnp.float32)).astype(jnp.bfloat16)
        result = lax.dot_general(third, high, NT_DIMS, preferred_element_type=jnp.float32)
        result = (
            result[: 2 * count]
            + result[2 * count :]
            + lax.dot_general(
                third[: 2 * count], low, NT_DIMS, preferred_element_type=jnp.float32
            )
        )
        for h in range(2):
            at = slice(h * LANES, (h + 1) * LANES)
            reals[pl.ds(station + h, count, stride=stations), :] = result[:count, at]
            imags[pl.ds(station + h, count, stride=stations), :] = result[count:, at]
    out_ref[:, :LANES] = reals[...].astype(jnp.bfloat16)
    out_ref[:, LANES:] = imags[...].astype(jnp.bfloat16)


def adjoint_kernel(panels, slots, n_src, chunk, *refs):
    packs = refs[:panels]
    observed_ref, green_ref, spectra_ref, other_ref, low_ref, out_ref = refs[panels : panels + 6]
    spectra, numbers, bank, green, mixed, total = refs[panels + 6 :]
    stations = spectra_ref.shape[0]
    panel = mixed.shape[0] // panels
    class_count = bank.shape[0]
    tiles = total.shape[0]
    blk_index = lax.axis_index("blk")
    for other in range(2):
        at = pl.ds(pl.multiple_of((blk_index ^ other) * LANES, LANES), LANES)
        lanes = slice(2 * other * LANES, 2 * (other + 1) * LANES)
        pair = observed_ref[:, :, at].astype(jnp.float32)
        pair = jnp.concatenate([pair[:, 0, :], pair[:, 1, :]], axis=1)
        bank[:, :, lanes] = jnp.broadcast_to(pair[:, None, :], (class_count, 8, 2 * LANES))
        pair = green_ref[:, :, at].astype(jnp.float32)
        pair = jnp.concatenate([pair[:, 0, :], pair[:, 1, :]], axis=1)
        green[:, lanes] = pair.astype(jnp.bfloat16)
    for k, pack in enumerate(packs):
        ids = pack[panel : panel + 16, :LANES].astype(jnp.int32)
        for row in range(2):
            numbers[k, row : row + 1] = jnp.concatenate(
                [ids[8 * row + slot : 8 * row + slot + 1, :panel] for slot in range(slots)], axis=1
            )
    spectra[:, : 2 * LANES] = spectra_ref[...]
    spectra[:, 2 * LANES :] = other_ref[...]
    widened = spectra[...].astype(jnp.float32)
    squares = jnp.sum(widened * widened, axis=0, keepdims=True)
    lanes = [slice(part * LANES, (part + 1) * LANES) for part in range(4)]
    power = []
    for real, imag in (lanes[:2], lanes[2:]):
        power += [squares[:, real] + squares[:, imag]] * 2
    power = jnp.concatenate(power, axis=1)
    green_ids = lax.broadcasted_iota(jnp.int32, (green.shape[0], slots * panel), 0)
    tile_ids = lax.broadcasted_iota(jnp.int32, (tiles, slots * panel), 0)
    class_ids = lax.broadcasted_iota(jnp.int32, (class_count, chunk, stations), 0)
    class_ids = class_ids.astype(jnp.float32).astype(jnp.bfloat16)
    total[...] = jnp.zeros_like(total)

    def mix(place):
        for start in range(0, panel, chunk):
            rows = packs[place][start : start + chunk]
            hot = jnp.where(rows[None] == class_ids, jnp.bfloat16(1.0), jnp.bfloat16(0.0))
            grouped = jnp.dot(
                hot.reshape(class_count * chunk, stations),
                spectra[...],
                preferred_element_type=jnp.float32,
            ).reshape(class_count, chunk // 8, 8, 4 * LANES)
            at = slice(place * panel + start, place * panel + start + chunk)
            for real, imag in (lanes[:2], lanes[2:]):
                obs_real, obs_imag = bank[:, :, real][:, None], bank[:, :, imag][:, None]
                group_real, group_imag = grouped[..., real], grouped[..., imag]
                mixed[at, real] = jnp.sum(
                    obs_real * group_real - obs_imag * group_imag, axis=0
                ).reshape(chunk, LANES)
                mixed[at, imag] = jnp.sum(
                    obs_real * group_imag + obs_imag * group_real, axis=0
                ).reshape(chunk, LANES)

    def gather(place):
        at = pl.ds(pl.multiple_of(place * panel, panel), panel)
        owner = blk_index ^ (2 * place)
        own = spectra[pl.ds(pl.multiple_of(owner * panel, panel), panel), :].astype(jnp.float32)
        adjoint = (own * power - mixed[at, :]) * (1.0 / stations)
        ids = numbers[place]
        pick = jnp.where(ids[:1] == green_ids, 1.0, 0.0).astype(jnp.bfloat16)
        tile = jnp.where(ids[1:2] == tile_ids, 1.0, 0.0).astype(jnp.bfloat16)
        all_picked = lax.dot_general(
            pick, green[...], TN_DIMS, preferred_element_type=jnp.float32
        )
        weighted = []
        for slot in range(slots):
            picked = all_picked[slot * panel : (slot + 1) * panel]
            row = []
            for real, imag in (lanes[:2], lanes[2:]):
                row.append(adjoint[:, real] * picked[:, real] + adjoint[:, imag] * picked[:, imag])
                row.append(adjoint[:, real] * picked[:, imag] - adjoint[:, imag] * picked[:, real])
            weighted.append(jnp.concatenate(row, axis=1).astype(jnp.bfloat16))
        total[...] += jnp.dot(
            tile,
            jnp.concatenate(weighted, axis=0),
            preferred_element_type=jnp.float32,
        )

    mix(0)
    for place in range(1, panels):
        mix(place)
        gather(place - 1)
    gather(panels - 1)
    low = [
        jnp.dot(
            total[:, at], low_ref[...], precision=HIGHEST, preferred_element_type=jnp.float32
        )
        for at in (slice(0, 2 * LANES), slice(2 * LANES, 4 * LANES))
    ]
    rows = []
    for owner in range(n_src):
        for other in range(2):
            for half in range(2):
                at = owner * (tiles // n_src) + 2 * half
                for part in range(4):
                    side = slice(part * TILE_SIDE, (part + 1) * TILE_SIDE)
                    rows.append(
                        jnp.concatenate(
                            [low[other][at : at + 1, side], low[other][at + 1 : at + 2, side]], axis=1
                        )
                    )
    rows = jnp.concatenate(rows, axis=0).astype(out_ref.dtype)
    for copy in range(out_ref.shape[0] // rows.shape[0]):
        out_ref[copy * 16 * n_src : (copy + 1) * 16 * n_src, :] = rows


def image_kernel(high_ref, parts_ref, out_ref):
    high = high_ref[lax.axis_index("blk")]
    image = jnp.dot(high, parts_ref[...], preferred_element_type=jnp.float32)
    count = image.shape[0] // 2
    image = image[:count] + image[count:]
    rows = count // 2
    for tile in range(out_ref.shape[0]):
        half, side = tile // 2, tile % 2
        for row in range(rows):
            at = half * rows + row
            out_ref[tile : tile + 1, row * TILE_SIDE : (row + 1) * TILE_SIDE] = image[
                at : at + 1, side * TILE_SIDE : (side + 1) * TILE_SIDE
            ]


def swap(values, axis, distance):
    size = lax.axis_size(axis)
    return lax.ppermute(values, axis, [(i, i ^ distance) for i in range(size)])


def split_body(windows, observed, pair_class, green, green_index, tile_index):
    n_blk, n_src = lax.axis_size("blk"), lax.axis_size("src")
    src_index = lax.axis_index("src")
    panel, local = windows.shape
    stations = panel * n_blk
    slots = green_index.shape[0]
    tiles = TILE_DEV * n_src
    share = panel // n_src
    pieces = [
        lax.dynamic_slice_in_dim(windows, (src_index ^ k) * share, share, 0)
        for k in range(n_src)
    ]
    pieces = pieces[:1] + [swap(pieces[k], "src", k) for k in range(1, n_src)]

    def widen(ids):
        return jnp.pad(ids, ((0, 8 - slots), (0, stations - panel)))

    pack = jnp.concatenate([pair_class, widen(green_index), widen(tile_index)], axis=0).astype(
        jnp.bfloat16
    )
    packs = [pack] + [swap(pack, "blk", k) for k in range(2, n_blk, 2)]

    first, twiddle, third = forward_tables(n_src, n_blk)
    low, high = mode_tables(n_src, n_blk, math.sqrt(tiles / (stations * slots)))
    devices = n_blk * n_src
    params = pltpu.CompilerParams(vmem_limit_bytes=VMEM_BYTES)
    blocks = pl.pallas_call(
        functools.partial(spectra_kernel, n_src),
        out_shape=jax.ShapeDtypeStruct((devices * share, 2 * LANES), jnp.bfloat16),
        scratch_shapes=[
            pltpu.VMEM((share * NT // LANES, LANES), jnp.float32),
            pltpu.VMEM((devices * share, LANES), jnp.float32),
            pltpu.VMEM((devices * share, LANES), jnp.float32),
        ],
        compiler_params=params,
        name="spectra",
    )(*pieces, first, twiddle, third)
    spectra = lax.all_to_all(
        blocks.reshape(devices, share, 2 * LANES), BOTH, 0, 0, tiled=True
    ).reshape(stations, 2 * LANES)
    class_count = observed.shape[0]
    panels = n_blk // 2
    spectra, packs = lax.optimization_barrier((spectra, packs))
    parts = pl.pallas_call(
        functools.partial(adjoint_kernel, panels, slots, n_src, 16),
        out_shape=jax.ShapeDtypeStruct((16 * devices, 2 * TILE_SIDE), PARTS_TYPE),
        scratch_shapes=[
            pltpu.VMEM((stations, 4 * LANES), jnp.bfloat16),
            pltpu.VMEM((panels, 8, slots * panel), jnp.int32),
            pltpu.VMEM((class_count, 8, 4 * LANES), jnp.float32),
            pltpu.VMEM((green.shape[0], 4 * LANES), jnp.bfloat16),
            pltpu.VMEM((panels * panel, 4 * LANES), jnp.float32),
            pltpu.VMEM((tiles, 4 * LANES), jnp.float32),
        ],
        compiler_params=params,
        name="adjoint",
    )(*packs, observed, green, spectra, swap(spectra, "blk", 1), low)
    parts = lax.all_to_all(
        parts.reshape(devices, 16, 2 * TILE_SIDE), BOTH, 0, 0, tiled=True
    ).reshape(16 * devices, 2 * TILE_SIDE)
    return pl.pallas_call(
        image_kernel,
        out_shape=jax.ShapeDtypeStruct((TILE_DEV, TP // n_blk), jnp.float32),
        compiler_params=params,
        name="image",
    )(high, parts)


def solution(mesh):
    in_specs = (
        P("blk", "src"),
        P(None, None, "src"),
        P("blk", None),
        P(None, None, "src"),
        P(None, "blk"),
        P(None, "blk"),
    )
    out_specs = P("src", "blk")
    whole_lanes = mesh.size * LANES == F
    body = split_body if whole_lanes else general_body
    return jax.shard_map(body, mesh=mesh, in_specs=in_specs, out_specs=out_specs, check_vma=False)
```

```python
import functools
import math

import jax
import jax.numpy as jnp
import numpy as np
from jax import lax
from jax.experimental import pallas as pl
from jax.experimental.pallas import tpu as pltpu
from jax.sharding import PartitionSpec as P

NT = 8192
TILE_SIDE = 64
TILE_DEV = 4
F = 4096
TP = 4096


def trig_pair(phase_index, period):
    angle_rad = phase_index.astype(jnp.float32) * (2.0 * math.pi / period)
    return (jnp.cos(angle_rad), jnp.sin(angle_rad))


def dft_rows(count, freq_ids, period):
    amp_scale = 1.0 / math.sqrt(period)
    local_freqs = freq_ids.shape[0]
    high_ids = jnp.arange(count // 128, dtype=jnp.int32)
    low_ids = jnp.arange(128, dtype=jnp.int32)
    high_cos, high_sin = trig_pair(high_ids[:, None] * 128 * freq_ids[None, :] % period, period)
    low_cos, low_sin = trig_pair(low_ids[:, None] * freq_ids[None, :] % period, period)
    cos_part = (
        high_cos[:, None, :] * low_cos[None] - high_sin[:, None, :] * low_sin[None]
    ).reshape(count, local_freqs)
    sin_part = (
        high_sin[:, None, :] * low_cos[None] + high_cos[:, None, :] * low_sin[None]
    ).reshape(count, local_freqs)
    return jnp.concatenate([cos_part * amp_scale, -sin_part * amp_scale], axis=1).astype(
        jnp.bfloat16
    )


def mode_table(freq_ids, points, edge_cells):
    phase_index = freq_ids[:, None] % edge_cells * (points[None, :] % edge_cells) + freq_ids[
        :, None
    ] // edge_cells * (points[None, :] // edge_cells)
    angle_rad = (phase_index % edge_cells).astype(jnp.float32) * (2.0 * math.pi / edge_cells)
    return jnp.concatenate([jnp.cos(angle_rad), -jnp.sin(angle_rad)], axis=0)


def general_body(windows, observed, pair_class, green, green_index, tile_index):
    panel_rows = windows.shape[0]
    local_freqs = observed.shape[2]
    class_count = observed.shape[0]
    src_index = lax.axis_index("src")
    blk_index = lax.axis_index("blk")
    stations = panel_rows * lax.axis_size("blk")
    freq_ids = src_index * local_freqs + jnp.arange(local_freqs, dtype=jnp.int32)
    shard_piece = lax.all_gather(windows, "src", axis=1, tiled=True)
    table_rows = dft_rows(shard_piece.shape[1], freq_ids, NT)
    spectra = jnp.dot(shard_piece, table_rows, preferred_element_type=jnp.float32).astype(
        jnp.bfloat16
    )
    class_ids = jnp.arange(class_count, dtype=jnp.int32)
    shard_piece = lax.all_gather(spectra, "blk", axis=0, tiled=True)
    widened = shard_piece.astype(jnp.float32)
    far_real = widened[:, :local_freqs]
    far_imag = widened[:, local_freqs:]
    power_sum = jnp.sum(far_real * far_real + far_imag * far_imag, axis=0)
    class_hot = (pair_class[:, :, None] == class_ids).astype(jnp.bfloat16)
    grouped = jnp.einsum("ijk,jf->ikf", class_hot, shard_piece, preferred_element_type=jnp.float32)
    power_sum, grouped = (power_sum, grouped)
    obs_table = observed.reshape(class_count, 2 * local_freqs).astype(jnp.float32)
    obs_real, obs_imag = (obs_table[:, :local_freqs], obs_table[:, local_freqs:])
    group_real, group_imag = (grouped[..., :local_freqs], grouped[..., local_freqs:])
    highest = lax.Precision.HIGHEST
    mix_real = jnp.einsum("kf,ikf->if", obs_real, group_real, precision=highest) - jnp.einsum(
        "kf,ikf->if", obs_imag, group_imag, precision=highest
    )
    mix_imag = jnp.einsum("kf,ikf->if", obs_real, group_imag, precision=highest) + jnp.einsum(
        "kf,ikf->if", obs_imag, group_real, precision=highest
    )
    own_spectra = spectra.astype(jnp.float32)
    adjoint = (
        own_spectra * jnp.concatenate([power_sum, power_sum])[None, :]
        - jnp.concatenate([mix_real, mix_imag], axis=1)
    ) / stations
    adj_real, adj_imag = (adjoint[:, :local_freqs], adjoint[:, local_freqs:])
    green_bank = green.reshape(green.shape[0], 2 * local_freqs)
    green_ids = jnp.arange(green_bank.shape[0], dtype=jnp.int32)
    pick_hot = (green_index[:, :, None] == green_ids).astype(jnp.bfloat16)
    picked = jnp.einsum(
        "npg,gf->npf", pick_hot, green_bank, preferred_element_type=jnp.bfloat16
    ).astype(jnp.float32)
    pick_real, pick_imag = (picked[..., :local_freqs], picked[..., local_freqs:])
    weighted = jnp.concatenate(
        [
            adj_real[None] * pick_real + adj_imag[None] * pick_imag,
            adj_real[None] * pick_imag - adj_imag[None] * pick_real,
        ],
        axis=-1,
    ).astype(jnp.bfloat16)
    tiles_all = TILE_DEV * lax.axis_size("src")
    tile_hot = (tile_index[:, :, None] == jnp.arange(tiles_all, dtype=jnp.int32)).astype(
        jnp.bfloat16
    )
    tile_spectra = jnp.einsum(
        "npt,npf->tf", tile_hot, weighted, preferred_element_type=jnp.float32
    ) * math.sqrt(tiles_all / (stations * green_index.shape[0]))
    summed = lax.psum(tile_spectra, "blk")
    point_share = TP // lax.axis_size("blk")
    points = blk_index * point_share + jnp.arange(point_share, dtype=jnp.int32)
    tile_image = jnp.dot(
        summed, mode_table(freq_ids, points, TILE_SIDE), precision=lax.Precision.HIGHEST
    ) / math.sqrt(F)
    return lax.psum_scatter(tile_image, "src", scatter_dimension=0, tiled=True)

LANES = 128
BOTH = ("blk", "src")
HIGHEST = lax.Precision.HIGHEST
NT_DIMS = (((1,), (1,)), ((), ()))
TN_DIMS = (((0,), (0,)), ((), ()))
VMEM_BYTES = 20 * 1024 * 1024
PARTS_TYPE = jnp.bfloat16


def split_bf16(values):
    high = values.astype(jnp.bfloat16)
    low = (values - high.astype(np.float32)).astype(jnp.bfloat16)
    return high, low


def forward_tables(n_src, n_blk):
    steps = NT // LANES
    rows = np.arange(steps)
    angle = 2 * np.pi / steps * ((rows[:, None] * rows[None, :]) % steps)
    first = np.concatenate([np.cos(angle), -np.sin(angle)], axis=0).astype(np.float32)
    first = np.concatenate(split_bf16(first), axis=0)
    lanes = np.arange(LANES)
    angle = 2 * np.pi / NT * ((lanes[:, None] * lanes[None, :]) % NT)
    twiddle = np.stack([np.cos(angle), -np.sin(angle)]).astype(np.float32)
    devices = np.arange(n_src * n_blk)
    block = devices % n_src * n_blk + devices // n_src
    angle = 2 * np.pi / steps * ((block[:, None] * lanes[None, :]) % steps)
    cos, sin = np.cos(angle), np.sin(angle)
    third = np.concatenate(
        [np.concatenate([cos, sin], axis=1), np.concatenate([-sin, cos], axis=1)], axis=0
    )
    third = split_bf16((third / math.sqrt(NT)).astype(np.float32))
    return first, twiddle, np.concatenate(third, axis=0)


def mode_tables(n_src, n_blk, scale):
    side = np.arange(TILE_SIDE)
    angle = 2 * np.pi / TILE_SIDE * ((side[:, None] * side[None, :]) % TILE_SIDE)
    cos, sin = np.cos(angle), np.sin(angle)
    low = np.zeros((2, 2, TILE_SIDE, 2, 2, TILE_SIDE))
    for parity in range(2):
        low[0, parity, :, parity, 0] = cos
        low[0, parity, :, parity, 1] = sin
        low[1, parity, :, parity, 0] = -sin
        low[1, parity, :, parity, 1] = cos
    low = low.reshape(4 * TILE_SIDE, 4 * TILE_SIDE) * scale
    devices = np.arange(n_src * n_blk)
    block = np.stack(
        [devices % n_src * n_blk + ((devices // n_src) ^ other) for other in range(2)], axis=1
    )
    high_freqs = block[..., None] * 2 + np.arange(2)
    angle = 2 * np.pi / TILE_SIDE * ((side[:, None, None, None] * high_freqs[None]) % TILE_SIDE)
    part = np.stack([np.cos(angle), -np.sin(angle)], axis=-1).reshape(
        n_blk, TILE_SIDE // n_blk, n_src * n_blk, 2, 4
    )
    high = np.zeros((n_blk, 2, TILE_SIDE // n_blk, n_src * n_blk, 2, 2, 4))
    for half in range(2):
        high[:, half, :, :, :, half] = part
    high = high.reshape(n_blk, 2 * TILE_SIDE // n_blk, 16 * n_src * n_blk)
    high = split_bf16((high / math.sqrt(F)).astype(np.float32))
    return low.astype(np.float32), np.concatenate(high, axis=1)


def spectra_kernel(n_src, *refs):
    pieces = refs[:n_src]
    first_ref, twiddle_ref, third_ref, out_ref, samples, reals, imags = refs[n_src:]
    stations, local = pieces[1].shape
    src_index = lax.axis_index("src")
    per_src = local // LANES
    steps = per_src * n_src
    count = third_ref.shape[0] // 4
    first = first_ref[...]
    for k in range(n_src):
        start = (src_index ^ k) * per_src
        for a in range(per_src):
            samples[pl.ds(start + a, stations, stride=steps), :] = pieces[k][
                :, a * LANES : (a + 1) * LANES
            ].astype(jnp.float32)
    twiddle_real, twiddle_imag = twiddle_ref[0], twiddle_ref[1]
    third = third_ref[...]
    for station in range(0, stations, 2):
        rows = jnp.concatenate(
            [samples[(station + h) * steps : (station + h + 1) * steps, :] for h in range(2)], axis=1
        ).astype(jnp.bfloat16)
        parts = jnp.dot(first, rows, preferred_element_type=jnp.float32)
        reals_here = parts[:steps] + parts[2 * steps : 3 * steps]
        imags_here = parts[steps : 2 * steps] + parts[3 * steps :]
        turned = []
        for h in range(2):
            at = slice(h * LANES, (h + 1) * LANES)
            real = jnp.concatenate([reals_here[:, at]] * (LANES // steps), axis=0)
            imag = jnp.concatenate([imags_here[:, at]] * (LANES // steps), axis=0)
            turned.append(
                jnp.concatenate(
                    [
                        real * twiddle_real - imag * twiddle_imag,
                        real * twiddle_imag + imag * twiddle_real,
                    ],
                    axis=1,
                )
            )
        turned = jnp.concatenate(turned, axis=0)
        high = turned.astype(jnp.bfloat16)
        low = (turned - high.astype(jnp.float32)).astype(jnp.bfloat16)
        result = lax.dot_general(third, high, NT_DIMS, preferred_element_type=jnp.float32)
        result = (
            result[: 2 * count]
            + result[2 * count :]
            + lax.dot_general(
                third[: 2 * count], low, NT_DIMS, preferred_element_type=jnp.float32
            )
        )
        for h in range(2):
            at = slice(h * LANES, (h + 1) * LANES)
            reals[pl.ds(station + h, count, stride=stations), :] = result[:count, at]
            imags[pl.ds(station + h, count, stride=stations), :] = result[count:, at]
    out_ref[:, :LANES] = reals[...].astype(jnp.bfloat16)
    out_ref[:, LANES:] = imags[...].astype(jnp.bfloat16)


def bank_kernel(observed_ref, green_ref, bank_ref, bank_green_ref):
    for other in range(2):
        at = pl.ds(pl.multiple_of((lax.axis_index("blk") ^ other) * LANES, LANES), LANES)
        lanes = slice(2 * other * LANES, 2 * (other + 1) * LANES)
        pair = observed_ref[:, :, at].astype(jnp.float32)
        pair = jnp.concatenate([pair[:, 0, :], pair[:, 1, :]], axis=1)
        bank_ref[:, :, lanes] = jnp.broadcast_to(
            pair[:, None, :], (pair.shape[0], 8, 2 * LANES)
        )
        pair = green_ref[:, :, at].astype(jnp.float32)
        pair = jnp.concatenate([pair[:, 0, :], pair[:, 1, :]], axis=1)
        bank_green_ref[:, lanes] = pair.astype(jnp.bfloat16)


def pick_kernel(slots, *refs):
    *packs, green_ref, picked_ref, tile_ref = refs
    panel = picked_ref.shape[1] // slots
    green_ids = lax.broadcasted_iota(jnp.int32, (green_ref.shape[0], slots * panel), 0)
    tile_ids = lax.broadcasted_iota(jnp.int32, (tile_ref.shape[1], slots * panel), 0)
    for k, pack in enumerate(packs):
        ids = pack[panel : panel + 16, :LANES].astype(jnp.int32)
        picks, seats = (
            jnp.concatenate([ids[row + slot : row + slot + 1, :panel] for slot in range(slots)], axis=1)
            for row in (0, 8)
        )
        picked_ref[k] = lax.dot_general(
            jnp.where(picks == green_ids, 1.0, 0.0).astype(jnp.bfloat16),
            green_ref[...],
            TN_DIMS,
            preferred_element_type=jnp.float32,
        ).astype(jnp.bfloat16)
        tile_ref[k] = jnp.where(seats == tile_ids, 1.0, 0.0).astype(jnp.bfloat16)


def adjoint_kernel(panels, slots, n_src, chunk, *refs):
    packs = refs[:panels]
    picked_ref, tile_ref, bank, spectra_ref, other_ref, low_ref, out_ref = refs[panels : panels + 7]
    spectra, mixed, total = refs[panels + 7 :]
    stations = spectra_ref.shape[0]
    panel = mixed.shape[0] // panels
    class_count = bank.shape[0]
    tiles = total.shape[0]
    blk_index = lax.axis_index("blk")
    spectra[:, : 2 * LANES] = spectra_ref[...]
    spectra[:, 2 * LANES :] = other_ref[...]
    widened = spectra[...].astype(jnp.float32)
    squares = jnp.sum(widened * widened, axis=0, keepdims=True)
    lanes = [slice(part * LANES, (part + 1) * LANES) for part in range(4)]
    power = []
    for real, imag in (lanes[:2], lanes[2:]):
        power += [squares[:, real] + squares[:, imag]] * 2
    power = jnp.concatenate(power, axis=1)
    class_ids = lax.broadcasted_iota(jnp.int32, (class_count, chunk, stations), 0)
    class_ids = class_ids.astype(jnp.float32).astype(jnp.bfloat16)
    total[...] = jnp.zeros_like(total)

    def mix(place):
        for start in range(0, panel, chunk):
            rows = packs[place][start : start + chunk]
            hot = jnp.where(rows[None] == class_ids, jnp.bfloat16(1.0), jnp.bfloat16(0.0))
            grouped = jnp.dot(
                hot.reshape(class_count * chunk, stations),
                spectra[...],
                preferred_element_type=jnp.float32,
            ).reshape(class_count, chunk // 8, 8, 4 * LANES)
            at = slice(place * panel + start, place * panel + start + chunk)
            for real, imag in (lanes[:2], lanes[2:]):
                obs_real, obs_imag = bank[:, :, real][:, None], bank[:, :, imag][:, None]
                group_real, group_imag = grouped[..., real], grouped[..., imag]
                mixed[at, real] = jnp.sum(
                    obs_real * group_real - obs_imag * group_imag, axis=0
                ).reshape(chunk, LANES)
                mixed[at, imag] = jnp.sum(
                    obs_real * group_imag + obs_imag * group_real, axis=0
                ).reshape(chunk, LANES)

    def gather(place):
        at = pl.ds(pl.multiple_of(place * panel, panel), panel)
        owner = blk_index ^ (2 * place)
        own = spectra[pl.ds(pl.multiple_of(owner * panel, panel), panel), :].astype(jnp.float32)
        adjoint = (own * power - mixed[at, :]) * (1.0 / stations)
        weighted = []
        for slot in range(slots):
            picked = picked_ref[place, slot * panel : (slot + 1) * panel].astype(jnp.float32)
            row = []
            for real, imag in (lanes[:2], lanes[2:]):
                row.append(adjoint[:, real] * picked[:, real] + adjoint[:, imag] * picked[:, imag])
                row.append(adjoint[:, real] * picked[:, imag] - adjoint[:, imag] * picked[:, real])
            weighted.append(jnp.concatenate(row, axis=1).astype(jnp.bfloat16))
        total[...] += jnp.dot(
            tile_ref[place],
            jnp.concatenate(weighted, axis=0),
            preferred_element_type=jnp.float32,
        )

    mix(0)
    for place in range(1, panels):
        mix(place)
        gather(place - 1)
    gather(panels - 1)
    low = [
        jnp.dot(
            total[:, at], low_ref[...], precision=HIGHEST, preferred_element_type=jnp.float32
        )
        for at in (slice(0, 2 * LANES), slice(2 * LANES, 4 * LANES))
    ]
    rows = []
    for owner in range(n_src):
        for other in range(2):
            for half in range(2):
                at = owner * (tiles // n_src) + 2 * half
                for part in range(4):
                    side = slice(part * TILE_SIDE, (part + 1) * TILE_SIDE)
                    rows.append(
                        jnp.concatenate(
                            [low[other][at : at + 1, side], low[other][at + 1 : at + 2, side]], axis=1
                        )
                    )
    rows = jnp.concatenate(rows, axis=0).astype(out_ref.dtype)
    for copy in range(out_ref.shape[0] // rows.shape[0]):
        out_ref[copy * 16 * n_src : (copy + 1) * 16 * n_src, :] = rows


def image_kernel(high_ref, parts_ref, out_ref):
    high = high_ref[lax.axis_index("blk")]
    image = jnp.dot(high, parts_ref[...], preferred_element_type=jnp.float32)
    count = image.shape[0] // 2
    image = image[:count] + image[count:]
    rows = count // 2
    for tile in range(out_ref.shape[0]):
        half, side = tile // 2, tile % 2
        for row in range(rows):
            at = half * rows + row
            out_ref[tile : tile + 1, row * TILE_SIDE : (row + 1) * TILE_SIDE] = image[
                at : at + 1, side * TILE_SIDE : (side + 1) * TILE_SIDE
            ]


def swap(values, axis, distance):
    size = lax.axis_size(axis)
    return lax.ppermute(values, axis, [(i, i ^ distance) for i in range(size)])


def split_body(windows, observed, pair_class, green, green_index, tile_index):
    n_blk, n_src = lax.axis_size("blk"), lax.axis_size("src")
    src_index = lax.axis_index("src")
    panel, local = windows.shape
    stations = panel * n_blk
    slots = green_index.shape[0]
    tiles = TILE_DEV * n_src
    share = panel // n_src
    pieces = [
        lax.dynamic_slice_in_dim(windows, (src_index ^ k) * share, share, 0)
        for k in range(n_src)
    ]
    pieces = pieces[:1] + [swap(pieces[k], "src", k) for k in range(1, n_src)]

    def widen(ids):
        return jnp.pad(ids, ((0, 8 - slots), (0, stations - panel)))

    pack = jnp.concatenate([pair_class, widen(green_index), widen(tile_index)], axis=0).astype(
        jnp.bfloat16
    )
    packs = [pack] + [swap(pack, "blk", k) for k in range(2, n_blk, 2)]

    first, twiddle, third = forward_tables(n_src, n_blk)
    low, high = mode_tables(n_src, n_blk, math.sqrt(tiles / (stations * slots)))
    devices = n_blk * n_src
    params = pltpu.CompilerParams(vmem_limit_bytes=VMEM_BYTES)
    banks = pl.pallas_call(
        bank_kernel,
        out_shape=(
            jax.ShapeDtypeStruct((observed.shape[0], 8, 4 * LANES), jnp.float32),
            jax.ShapeDtypeStruct((green.shape[0], 4 * LANES), jnp.bfloat16),
        ),
        compiler_params=params,
        name="bank",
    )(observed, green)
    pieces, banks = lax.optimization_barrier((pieces, banks))
    blocks = pl.pallas_call(
        functools.partial(spectra_kernel, n_src),
        out_shape=jax.ShapeDtypeStruct((devices * share, 2 * LANES), jnp.bfloat16),
        scratch_shapes=[
            pltpu.VMEM((share * NT // LANES, LANES), jnp.float32),
            pltpu.VMEM((devices * share, LANES), jnp.float32),
            pltpu.VMEM((devices * share, LANES), jnp.float32),
        ],
        compiler_params=params,
        name="spectra",
    )(*pieces, first, twiddle, third)
    spectra = lax.all_to_all(
        blocks.reshape(devices, share, 2 * LANES), BOTH, 0, 0, tiled=True
    ).reshape(stations, 2 * LANES)
    class_count = observed.shape[0]
    panels = n_blk // 2
    spectra, packs = lax.optimization_barrier((spectra, packs))
    picked, tile = pl.pallas_call(
        functools.partial(pick_kernel, slots),
        out_shape=(
            jax.ShapeDtypeStruct((panels, slots * panel, 4 * LANES), jnp.bfloat16),
            jax.ShapeDtypeStruct((panels, tiles, slots * panel), jnp.bfloat16),
        ),
        compiler_params=params,
        name="pick",
    )(*packs, banks[1])
    parts = pl.pallas_call(
        functools.partial(adjoint_kernel, panels, slots, n_src, 16),
        out_shape=jax.ShapeDtypeStruct((16 * devices, 2 * TILE_SIDE), PARTS_TYPE),
        scratch_shapes=[
            pltpu.VMEM((stations, 4 * LANES), jnp.bfloat16),
            pltpu.VMEM((panels * panel, 4 * LANES), jnp.float32),
            pltpu.VMEM((tiles, 4 * LANES), jnp.float32),
        ],
        compiler_params=params,
        name="adjoint",
    )(*packs, picked, tile, banks[0], spectra, swap(spectra, "blk", 1), low)
    parts = lax.all_to_all(
        parts.reshape(devices, 16, 2 * TILE_SIDE), BOTH, 0, 0, tiled=True
    ).reshape(16 * devices, 2 * TILE_SIDE)
    return pl.pallas_call(
        image_kernel,
        out_shape=jax.ShapeDtypeStruct((TILE_DEV, TP // n_blk), jnp.float32),
        compiler_params=params,
        name="image",
    )(high, parts)


def solution(mesh):
    in_specs = (
        P("blk", "src"),
        P(None, None, "src"),
        P("blk", None),
        P(None, None, "src"),
        P(None, "blk"),
        P(None, "blk"),
    )
    out_specs = P("src", "blk")
    whole_lanes = mesh.size * LANES == F
    body = split_body if whole_lanes else general_body
    return jax.shard_map(body, mesh=mesh, in_specs=in_specs, out_specs=out_specs, check_vma=False)
```

```python
import functools
import math

import jax
import jax.numpy as jnp
import numpy as np
from jax import lax
from jax.experimental import pallas as pl
from jax.experimental.pallas import tpu as pltpu
from jax.sharding import PartitionSpec as P

NT = 8192
TILE_SIDE = 64
TILE_DEV = 4
F = 4096
TP = 4096


def trig_pair(phase_index, period):
    angle_rad = phase_index.astype(jnp.float32) * (2.0 * math.pi / period)
    return (jnp.cos(angle_rad), jnp.sin(angle_rad))


def dft_rows(count, freq_ids, period):
    amp_scale = 1.0 / math.sqrt(period)
    local_freqs = freq_ids.shape[0]
    high_ids = jnp.arange(count // 128, dtype=jnp.int32)
    low_ids = jnp.arange(128, dtype=jnp.int32)
    high_cos, high_sin = trig_pair(high_ids[:, None] * 128 * freq_ids[None, :] % period, period)
    low_cos, low_sin = trig_pair(low_ids[:, None] * freq_ids[None, :] % period, period)
    cos_part = (
        high_cos[:, None, :] * low_cos[None] - high_sin[:, None, :] * low_sin[None]
    ).reshape(count, local_freqs)
    sin_part = (
        high_sin[:, None, :] * low_cos[None] + high_cos[:, None, :] * low_sin[None]
    ).reshape(count, local_freqs)
    return jnp.concatenate([cos_part * amp_scale, -sin_part * amp_scale], axis=1).astype(
        jnp.bfloat16
    )


def mode_table(freq_ids, points, edge_cells):
    phase_index = freq_ids[:, None] % edge_cells * (points[None, :] % edge_cells) + freq_ids[
        :, None
    ] // edge_cells * (points[None, :] // edge_cells)
    angle_rad = (phase_index % edge_cells).astype(jnp.float32) * (2.0 * math.pi / edge_cells)
    return jnp.concatenate([jnp.cos(angle_rad), -jnp.sin(angle_rad)], axis=0)


def general_body(windows, observed, pair_class, green, green_index, tile_index):
    panel_rows = windows.shape[0]
    local_freqs = observed.shape[2]
    class_count = observed.shape[0]
    src_index = lax.axis_index("src")
    blk_index = lax.axis_index("blk")
    stations = panel_rows * lax.axis_size("blk")
    freq_ids = src_index * local_freqs + jnp.arange(local_freqs, dtype=jnp.int32)
    shard_piece = lax.all_gather(windows, "src", axis=1, tiled=True)
    table_rows = dft_rows(shard_piece.shape[1], freq_ids, NT)
    spectra = jnp.dot(shard_piece, table_rows, preferred_element_type=jnp.float32).astype(
        jnp.bfloat16
    )
    class_ids = jnp.arange(class_count, dtype=jnp.int32)
    shard_piece = lax.all_gather(spectra, "blk", axis=0, tiled=True)
    widened = shard_piece.astype(jnp.float32)
    far_real = widened[:, :local_freqs]
    far_imag = widened[:, local_freqs:]
    power_sum = jnp.sum(far_real * far_real + far_imag * far_imag, axis=0)
    class_hot = (pair_class[:, :, None] == class_ids).astype(jnp.bfloat16)
    grouped = jnp.einsum("ijk,jf->ikf", class_hot, shard_piece, preferred_element_type=jnp.float32)
    power_sum, grouped = (power_sum, grouped)
    obs_table = observed.reshape(class_count, 2 * local_freqs).astype(jnp.float32)
    obs_real, obs_imag = (obs_table[:, :local_freqs], obs_table[:, local_freqs:])
    group_real, group_imag = (grouped[..., :local_freqs], grouped[..., local_freqs:])
    highest = lax.Precision.HIGHEST
    mix_real = jnp.einsum("kf,ikf->if", obs_real, group_real, precision=highest) - jnp.einsum(
        "kf,ikf->if", obs_imag, group_imag, precision=highest
    )
    mix_imag = jnp.einsum("kf,ikf->if", obs_real, group_imag, precision=highest) + jnp.einsum(
        "kf,ikf->if", obs_imag, group_real, precision=highest
    )
    own_spectra = spectra.astype(jnp.float32)
    adjoint = (
        own_spectra * jnp.concatenate([power_sum, power_sum])[None, :]
        - jnp.concatenate([mix_real, mix_imag], axis=1)
    ) / stations
    adj_real, adj_imag = (adjoint[:, :local_freqs], adjoint[:, local_freqs:])
    green_bank = green.reshape(green.shape[0], 2 * local_freqs)
    green_ids = jnp.arange(green_bank.shape[0], dtype=jnp.int32)
    pick_hot = (green_index[:, :, None] == green_ids).astype(jnp.bfloat16)
    picked = jnp.einsum(
        "npg,gf->npf", pick_hot, green_bank, preferred_element_type=jnp.bfloat16
    ).astype(jnp.float32)
    pick_real, pick_imag = (picked[..., :local_freqs], picked[..., local_freqs:])
    weighted = jnp.concatenate(
        [
            adj_real[None] * pick_real + adj_imag[None] * pick_imag,
            adj_real[None] * pick_imag - adj_imag[None] * pick_real,
        ],
        axis=-1,
    ).astype(jnp.bfloat16)
    tiles_all = TILE_DEV * lax.axis_size("src")
    tile_hot = (tile_index[:, :, None] == jnp.arange(tiles_all, dtype=jnp.int32)).astype(
        jnp.bfloat16
    )
    tile_spectra = jnp.einsum(
        "npt,npf->tf", tile_hot, weighted, preferred_element_type=jnp.float32
    ) * math.sqrt(tiles_all / (stations * green_index.shape[0]))
    summed = lax.psum(tile_spectra, "blk")
    point_share = TP // lax.axis_size("blk")
    points = blk_index * point_share + jnp.arange(point_share, dtype=jnp.int32)
    tile_image = jnp.dot(
        summed, mode_table(freq_ids, points, TILE_SIDE), precision=lax.Precision.HIGHEST
    ) / math.sqrt(F)
    return lax.psum_scatter(tile_image, "src", scatter_dimension=0, tiled=True)

LANES = 128
BOTH = ("blk", "src")
HIGHEST = lax.Precision.HIGHEST
NT_DIMS = (((1,), (1,)), ((), ()))
TN_DIMS = (((0,), (0,)), ((), ()))
VMEM_BYTES = 20 * 1024 * 1024
PARTS_TYPE = jnp.bfloat16


def split_bf16(values):
    high = values.astype(jnp.bfloat16)
    low = (values - high.astype(np.float32)).astype(jnp.bfloat16)
    return high, low


def forward_tables(n_src, n_blk):
    steps = NT // LANES
    rows = np.arange(steps)
    angle = 2 * np.pi / steps * ((rows[:, None] * rows[None, :]) % steps)
    first = np.concatenate([np.cos(angle), -np.sin(angle)], axis=0).astype(np.float32)
    first = np.concatenate(split_bf16(first), axis=0)
    lanes = np.arange(LANES)
    angle = 2 * np.pi / NT * ((lanes[:, None] * lanes[None, :]) % NT)
    twiddle = np.stack([np.cos(angle), -np.sin(angle)]).astype(np.float32)
    devices = np.arange(n_src * n_blk)
    block = devices % n_src * n_blk + devices // n_src
    angle = 2 * np.pi / steps * ((block[:, None] * lanes[None, :]) % steps)
    cos, sin = np.cos(angle), np.sin(angle)
    third = np.concatenate(
        [np.concatenate([cos, sin], axis=1), np.concatenate([-sin, cos], axis=1)], axis=0
    )
    third = split_bf16((third / math.sqrt(NT)).astype(np.float32))
    return first, twiddle, np.concatenate(third, axis=0)


def mode_tables(n_src, n_blk, scale):
    side = np.arange(TILE_SIDE)
    angle = 2 * np.pi / TILE_SIDE * ((side[:, None] * side[None, :]) % TILE_SIDE)
    cos, sin = np.cos(angle), np.sin(angle)
    low = np.zeros((2, 2, TILE_SIDE, 2, 2, TILE_SIDE))
    for parity in range(2):
        low[0, parity, :, parity, 0] = cos
        low[0, parity, :, parity, 1] = sin
        low[1, parity, :, parity, 0] = -sin
        low[1, parity, :, parity, 1] = cos
    low = low.reshape(4 * TILE_SIDE, 4 * TILE_SIDE) * scale
    devices = np.arange(n_src * n_blk)
    block = np.stack(
        [devices % n_src * n_blk + ((devices // n_src) ^ other) for other in range(2)], axis=1
    )
    high_freqs = block[..., None] * 2 + np.arange(2)
    angle = 2 * np.pi / TILE_SIDE * ((side[:, None, None, None] * high_freqs[None]) % TILE_SIDE)
    part = np.stack([np.cos(angle), -np.sin(angle)], axis=-1).reshape(
        n_blk, TILE_SIDE // n_blk, n_src * n_blk, 2, 4
    )
    high = np.zeros((n_blk, 2, TILE_SIDE // n_blk, n_src * n_blk, 2, 2, 4))
    for half in range(2):
        high[:, half, :, :, :, half] = part
    high = high.reshape(n_blk, 2 * TILE_SIDE // n_blk, 16 * n_src * n_blk)
    high = split_bf16((high / math.sqrt(F)).astype(np.float32))
    low = np.concatenate(split_bf16(low.astype(np.float32)), axis=1)
    return low, np.concatenate(high, axis=1)


def spectra_kernel(n_src, *refs):
    pieces = refs[:n_src]
    first_ref, twiddle_ref, third_ref, out_ref, samples, reals, imags = refs[n_src:]
    stations, local = pieces[1].shape
    src_index = lax.axis_index("src")
    per_src = local // LANES
    steps = per_src * n_src
    count = third_ref.shape[0] // 4
    first = first_ref[...]
    for k in range(n_src):
        start = (src_index ^ k) * per_src
        for a in range(per_src):
            samples[pl.ds(start + a, stations, stride=steps), :] = pieces[k][
                :, a * LANES : (a + 1) * LANES
            ].astype(jnp.float32)
    twiddle_real, twiddle_imag = twiddle_ref[0], twiddle_ref[1]
    third = third_ref[...]
    for station in range(0, stations, 2):
        rows = jnp.concatenate(
            [samples[(station + h) * steps : (station + h + 1) * steps, :] for h in range(2)], axis=1
        ).astype(jnp.bfloat16)
        parts = jnp.dot(first, rows, preferred_element_type=jnp.float32)
        reals_here = parts[:steps] + parts[2 * steps : 3 * steps]
        imags_here = parts[steps : 2 * steps] + parts[3 * steps :]
        turned = []
        for h in range(2):
            at = slice(h * LANES, (h + 1) * LANES)
            real = jnp.concatenate([reals_here[:, at]] * (LANES // steps), axis=0)
            imag = jnp.concatenate([imags_here[:, at]] * (LANES // steps), axis=0)
            turned.append(
                jnp.concatenate(
                    [
                        real * twiddle_real - imag * twiddle_imag,
                        real * twiddle_imag + imag * twiddle_real,
                    ],
                    axis=1,
                )
            )
        turned = jnp.concatenate(turned, axis=0)
        high = turned.astype(jnp.bfloat16)
        low = (turned - high.astype(jnp.float32)).astype(jnp.bfloat16)
        result = lax.dot_general(third, high, NT_DIMS, preferred_element_type=jnp.float32)
        result = (
            result[: 2 * count]
            + result[2 * count :]
            + lax.dot_general(
                third[: 2 * count], low, NT_DIMS, preferred_element_type=jnp.float32
            )
        )
        for h in range(2):
            at = slice(h * LANES, (h + 1) * LANES)
            reals[pl.ds(station + h, count, stride=stations), :] = result[:count, at]
            imags[pl.ds(station + h, count, stride=stations), :] = result[count:, at]
    out_ref[:, :LANES] = reals[...].astype(jnp.bfloat16)
    out_ref[:, LANES:] = imags[...].astype(jnp.bfloat16)


def bank_kernel(observed_ref, green_ref, bank_ref, bank_green_ref):
    for other in range(2):
        at = pl.ds(pl.multiple_of((lax.axis_index("blk") ^ other) * LANES, LANES), LANES)
        lanes = slice(2 * other * LANES, 2 * (other + 1) * LANES)
        pair = observed_ref[:, :, at].astype(jnp.float32)
        pair = jnp.concatenate([pair[:, 0, :], pair[:, 1, :]], axis=1)
        bank_ref[:, :, lanes] = jnp.broadcast_to(
            pair[:, None, :], (pair.shape[0], 8, 2 * LANES)
        )
        pair = green_ref[:, :, at].astype(jnp.float32)
        pair = jnp.concatenate([pair[:, 0, :], pair[:, 1, :]], axis=1)
        bank_green_ref[:, lanes] = pair.astype(jnp.bfloat16)


def pick_kernel(slots, *refs):
    *packs, green_ref, picked_ref, tile_ref = refs
    panel = picked_ref.shape[1] // slots
    green_ids = lax.broadcasted_iota(jnp.int32, (green_ref.shape[0], slots * panel), 0)
    tile_ids = lax.broadcasted_iota(jnp.int32, (tile_ref.shape[1], slots * panel), 0)
    for k, pack in enumerate(packs):
        ids = pack[panel : panel + 16, :LANES].astype(jnp.int32)
        picks, seats = (
            jnp.concatenate([ids[row + slot : row + slot + 1, :panel] for slot in range(slots)], axis=1)
            for row in (0, 8)
        )
        picked_ref[k] = lax.dot_general(
            jnp.where(picks == green_ids, 1.0, 0.0).astype(jnp.bfloat16),
            green_ref[...],
            TN_DIMS,
            preferred_element_type=jnp.float32,
        ).astype(jnp.bfloat16)
        tile_ref[k] = jnp.where(seats == tile_ids, 1.0, 0.0).astype(jnp.bfloat16)


def three_pass(values, table_ref):
    width = table_ref.shape[1] // 2
    high = values.astype(jnp.bfloat16)
    low = (values - high.astype(jnp.float32)).astype(jnp.bfloat16)
    both = jnp.dot(high, table_ref[...], preferred_element_type=jnp.float32)
    rest = jnp.dot(low, table_ref[:, :width], preferred_element_type=jnp.float32)
    return both[:, :width] + both[:, width:] + rest


def adjoint_kernel(panels, slots, n_src, chunk, *refs):
    packs = refs[:panels]
    picked_ref, tile_ref, bank, spectra_ref, other_ref, low_ref, out_ref = refs[panels : panels + 7]
    spectra, mixed, total = refs[panels + 7 :]
    stations = spectra_ref.shape[0]
    panel = mixed.shape[0] // panels
    class_count = bank.shape[0]
    tiles = total.shape[0]
    blk_index = lax.axis_index("blk")
    spectra[:, : 2 * LANES] = spectra_ref[...]
    spectra[:, 2 * LANES :] = other_ref[...]
    widened = spectra[...].astype(jnp.float32)
    squares = jnp.sum(widened * widened, axis=0, keepdims=True)
    lanes = [slice(part * LANES, (part + 1) * LANES) for part in range(4)]
    power = []
    for real, imag in (lanes[:2], lanes[2:]):
        power += [squares[:, real] + squares[:, imag]] * 2
    power = jnp.concatenate(power, axis=1)
    class_ids = lax.broadcasted_iota(jnp.int32, (class_count, chunk, stations), 0)
    class_ids = class_ids.astype(jnp.float32).astype(jnp.bfloat16)
    total[...] = jnp.zeros_like(total)

    def mix(place):
        for start in range(0, panel, chunk):
            rows = packs[place][start : start + chunk]
            hot = jnp.where(rows[None] == class_ids, jnp.bfloat16(1.0), jnp.bfloat16(0.0))
            grouped = jnp.dot(
                hot.reshape(class_count * chunk, stations),
                spectra[...],
                preferred_element_type=jnp.float32,
            ).reshape(class_count, chunk // 8, 8, 4 * LANES)
            at = slice(place * panel + start, place * panel + start + chunk)
            for real, imag in (lanes[:2], lanes[2:]):
                obs_real, obs_imag = bank[:, :, real][:, None], bank[:, :, imag][:, None]
                group_real, group_imag = grouped[..., real], grouped[..., imag]
                mixed[at, real] = jnp.sum(
                    obs_real * group_real - obs_imag * group_imag, axis=0
                ).reshape(chunk, LANES)
                mixed[at, imag] = jnp.sum(
                    obs_real * group_imag + obs_imag * group_real, axis=0
                ).reshape(chunk, LANES)

    def gather(place):
        at = pl.ds(pl.multiple_of(place * panel, panel), panel)
        owner = blk_index ^ (2 * place)
        own = spectra[pl.ds(pl.multiple_of(owner * panel, panel), panel), :].astype(jnp.float32)
        adjoint = (own * power - mixed[at, :]) * (1.0 / stations)
        weighted = []
        for slot in range(slots):
            picked = picked_ref[place, slot * panel : (slot + 1) * panel].astype(jnp.float32)
            row = []
            for real, imag in (lanes[:2], lanes[2:]):
                row.append(adjoint[:, real] * picked[:, real] + adjoint[:, imag] * picked[:, imag])
                row.append(adjoint[:, real] * picked[:, imag] - adjoint[:, imag] * picked[:, real])
            weighted.append(jnp.concatenate(row, axis=1).astype(jnp.bfloat16))
        total[...] += jnp.dot(
            tile_ref[place],
            jnp.concatenate(weighted, axis=0),
            preferred_element_type=jnp.float32,
        )

    for place in range(panels):
        mix(place)
    for place in range(panels):
        gather(place)
    low = [
        three_pass(total[:, at], low_ref)
        for at in (slice(0, 2 * LANES), slice(2 * LANES, 4 * LANES))
    ]
    rows = []
    for owner in range(n_src):
        for other in range(2):
            for half in range(2):
                at = owner * (tiles // n_src) + 2 * half
                for part in range(4):
                    side = slice(part * TILE_SIDE, (part + 1) * TILE_SIDE)
                    rows.append(
                        jnp.concatenate(
                            [low[other][at : at + 1, side], low[other][at + 1 : at + 2, side]], axis=1
                        )
                    )
    rows = jnp.concatenate(rows, axis=0).astype(out_ref.dtype)
    for copy in range(out_ref.shape[0] // rows.shape[0]):
        out_ref[copy * 16 * n_src : (copy + 1) * 16 * n_src, :] = rows


def image_kernel(high_ref, parts_ref, out_ref):
    high = high_ref[lax.axis_index("blk")]
    image = jnp.dot(high, parts_ref[...], preferred_element_type=jnp.float32)
    count = image.shape[0] // 2
    image = image[:count] + image[count:]
    rows = count // 2
    for tile in range(out_ref.shape[0]):
        half, side = tile // 2, tile % 2
        for row in range(rows):
            at = half * rows + row
            out_ref[tile : tile + 1, row * TILE_SIDE : (row + 1) * TILE_SIDE] = image[
                at : at + 1, side * TILE_SIDE : (side + 1) * TILE_SIDE
            ]


def swap(values, axis, distance):
    size = lax.axis_size(axis)
    return lax.ppermute(values, axis, [(i, i ^ distance) for i in range(size)])


def split_body(windows, observed, pair_class, green, green_index, tile_index):
    n_blk, n_src = lax.axis_size("blk"), lax.axis_size("src")
    src_index = lax.axis_index("src")
    panel, local = windows.shape
    stations = panel * n_blk
    slots = green_index.shape[0]
    tiles = TILE_DEV * n_src
    share = panel // n_src
    pieces = [
        lax.dynamic_slice_in_dim(windows, (src_index ^ k) * share, share, 0)
        for k in range(n_src)
    ]
    pieces = pieces[:1] + [swap(pieces[k], "src", k) for k in range(1, n_src)]

    def widen(ids):
        return jnp.pad(ids, ((0, 8 - slots), (0, stations - panel)))

    pack = jnp.concatenate([pair_class, widen(green_index), widen(tile_index)], axis=0).astype(
        jnp.bfloat16
    )
    packs = [pack] + [swap(pack, "blk", k) for k in range(2, n_blk, 2)]

    first, twiddle, third = forward_tables(n_src, n_blk)
    low, high = mode_tables(n_src, n_blk, math.sqrt(tiles / (stations * slots)))
    devices = n_blk * n_src
    params = pltpu.CompilerParams(vmem_limit_bytes=VMEM_BYTES)
    banks = pl.pallas_call(
        bank_kernel,
        out_shape=(
            jax.ShapeDtypeStruct((observed.shape[0], 8, 4 * LANES), jnp.float32),
            jax.ShapeDtypeStruct((green.shape[0], 4 * LANES), jnp.bfloat16),
        ),
        compiler_params=params,
        name="bank",
    )(observed, green)
    pieces, banks = lax.optimization_barrier((pieces, banks))
    blocks = pl.pallas_call(
        functools.partial(spectra_kernel, n_src),
        out_shape=jax.ShapeDtypeStruct((devices * share, 2 * LANES), jnp.bfloat16),
        scratch_shapes=[
            pltpu.VMEM((share * NT // LANES, LANES), jnp.float32),
            pltpu.VMEM((devices * share, LANES), jnp.float32),
            pltpu.VMEM((devices * share, LANES), jnp.float32),
        ],
        compiler_params=params,
        name="spectra",
    )(*pieces, first, twiddle, third)
    spectra = lax.all_to_all(
        blocks.reshape(devices, share, 2 * LANES), BOTH, 0, 0, tiled=True
    ).reshape(stations, 2 * LANES)
    class_count = observed.shape[0]
    panels = n_blk // 2
    spectra, packs = lax.optimization_barrier((spectra, packs))
    picked, tile = pl.pallas_call(
        functools.partial(pick_kernel, slots),
        out_shape=(
            jax.ShapeDtypeStruct((panels, slots * panel, 4 * LANES), jnp.bfloat16),
            jax.ShapeDtypeStruct((panels, tiles, slots * panel), jnp.bfloat16),
        ),
        compiler_params=params,
        name="pick",
    )(*packs, banks[1])
    parts = pl.pallas_call(
        functools.partial(adjoint_kernel, panels, slots, n_src, 16),
        out_shape=jax.ShapeDtypeStruct((16 * devices, 2 * TILE_SIDE), PARTS_TYPE),
        scratch_shapes=[
            pltpu.VMEM((stations, 4 * LANES), jnp.bfloat16),
            pltpu.VMEM((panels * panel, 4 * LANES), jnp.float32),
            pltpu.VMEM((tiles, 4 * LANES), jnp.float32),
        ],
        compiler_params=params,
        name="adjoint",
    )(*packs, picked, tile, banks[0], spectra, swap(spectra, "blk", 1), low)
    parts = lax.all_to_all(
        parts.reshape(devices, 16, 2 * TILE_SIDE), BOTH, 0, 0, tiled=True
    ).reshape(16 * devices, 2 * TILE_SIDE)
    return pl.pallas_call(
        image_kernel,
        out_shape=jax.ShapeDtypeStruct((TILE_DEV, TP // n_blk), jnp.float32),
        compiler_params=params,
        name="image",
    )(high, parts)


def solution(mesh):
    in_specs = (
        P("blk", "src"),
        P(None, None, "src"),
        P("blk", None),
        P(None, None, "src"),
        P(None, "blk"),
        P(None, "blk"),
    )
    out_specs = P("src", "blk")
    whole_lanes = mesh.size * LANES == F
    body = split_body if whole_lanes else general_body
    return jax.shard_map(body, mesh=mesh, in_specs=in_specs, out_specs=out_specs, check_vma=False)
```

```python
import functools
import math

import jax
import jax.numpy as jnp
import numpy as np
from jax import lax
from jax.experimental import pallas as pl
from jax.experimental.pallas import tpu as pltpu
from jax.sharding import PartitionSpec as P

NT = 8192
TILE_SIDE = 64
TILE_DEV = 4
F = 4096
TP = 4096


def trig_pair(phase_index, period):
    angle_rad = phase_index.astype(jnp.float32) * (2.0 * math.pi / period)
    return (jnp.cos(angle_rad), jnp.sin(angle_rad))


def dft_rows(count, freq_ids, period):
    amp_scale = 1.0 / math.sqrt(period)
    local_freqs = freq_ids.shape[0]
    high_ids = jnp.arange(count // 128, dtype=jnp.int32)
    low_ids = jnp.arange(128, dtype=jnp.int32)
    high_cos, high_sin = trig_pair(high_ids[:, None] * 128 * freq_ids[None, :] % period, period)
    low_cos, low_sin = trig_pair(low_ids[:, None] * freq_ids[None, :] % period, period)
    cos_part = (
        high_cos[:, None, :] * low_cos[None] - high_sin[:, None, :] * low_sin[None]
    ).reshape(count, local_freqs)
    sin_part = (
        high_sin[:, None, :] * low_cos[None] + high_cos[:, None, :] * low_sin[None]
    ).reshape(count, local_freqs)
    return jnp.concatenate([cos_part * amp_scale, -sin_part * amp_scale], axis=1).astype(
        jnp.bfloat16
    )


def mode_table(freq_ids, points, edge_cells):
    phase_index = freq_ids[:, None] % edge_cells * (points[None, :] % edge_cells) + freq_ids[
        :, None
    ] // edge_cells * (points[None, :] // edge_cells)
    angle_rad = (phase_index % edge_cells).astype(jnp.float32) * (2.0 * math.pi / edge_cells)
    return jnp.concatenate([jnp.cos(angle_rad), -jnp.sin(angle_rad)], axis=0)


def general_body(windows, observed, pair_class, green, green_index, tile_index):
    panel_rows = windows.shape[0]
    local_freqs = observed.shape[2]
    class_count = observed.shape[0]
    src_index = lax.axis_index("src")
    blk_index = lax.axis_index("blk")
    stations = panel_rows * lax.axis_size("blk")
    freq_ids = src_index * local_freqs + jnp.arange(local_freqs, dtype=jnp.int32)
    shard_piece = lax.all_gather(windows, "src", axis=1, tiled=True)
    table_rows = dft_rows(shard_piece.shape[1], freq_ids, NT)
    spectra = jnp.dot(shard_piece, table_rows, preferred_element_type=jnp.float32).astype(
        jnp.bfloat16
    )
    class_ids = jnp.arange(class_count, dtype=jnp.int32)
    shard_piece = lax.all_gather(spectra, "blk", axis=0, tiled=True)
    widened = shard_piece.astype(jnp.float32)
    far_real = widened[:, :local_freqs]
    far_imag = widened[:, local_freqs:]
    power_sum = jnp.sum(far_real * far_real + far_imag * far_imag, axis=0)
    class_hot = (pair_class[:, :, None] == class_ids).astype(jnp.bfloat16)
    grouped = jnp.einsum("ijk,jf->ikf", class_hot, shard_piece, preferred_element_type=jnp.float32)
    power_sum, grouped = (power_sum, grouped)
    obs_table = observed.reshape(class_count, 2 * local_freqs).astype(jnp.float32)
    obs_real, obs_imag = (obs_table[:, :local_freqs], obs_table[:, local_freqs:])
    group_real, group_imag = (grouped[..., :local_freqs], grouped[..., local_freqs:])
    highest = lax.Precision.HIGHEST
    mix_real = jnp.einsum("kf,ikf->if", obs_real, group_real, precision=highest) - jnp.einsum(
        "kf,ikf->if", obs_imag, group_imag, precision=highest
    )
    mix_imag = jnp.einsum("kf,ikf->if", obs_real, group_imag, precision=highest) + jnp.einsum(
        "kf,ikf->if", obs_imag, group_real, precision=highest
    )
    own_spectra = spectra.astype(jnp.float32)
    adjoint = (
        own_spectra * jnp.concatenate([power_sum, power_sum])[None, :]
        - jnp.concatenate([mix_real, mix_imag], axis=1)
    ) / stations
    adj_real, adj_imag = (adjoint[:, :local_freqs], adjoint[:, local_freqs:])
    green_bank = green.reshape(green.shape[0], 2 * local_freqs)
    green_ids = jnp.arange(green_bank.shape[0], dtype=jnp.int32)
    pick_hot = (green_index[:, :, None] == green_ids).astype(jnp.bfloat16)
    picked = jnp.einsum(
        "npg,gf->npf", pick_hot, green_bank, preferred_element_type=jnp.bfloat16
    ).astype(jnp.float32)
    pick_real, pick_imag = (picked[..., :local_freqs], picked[..., local_freqs:])
    weighted = jnp.concatenate(
        [
            adj_real[None] * pick_real + adj_imag[None] * pick_imag,
            adj_real[None] * pick_imag - adj_imag[None] * pick_real,
        ],
        axis=-1,
    ).astype(jnp.bfloat16)
    tiles_all = TILE_DEV * lax.axis_size("src")
    tile_hot = (tile_index[:, :, None] == jnp.arange(tiles_all, dtype=jnp.int32)).astype(
        jnp.bfloat16
    )
    tile_spectra = jnp.einsum(
        "npt,npf->tf", tile_hot, weighted, preferred_element_type=jnp.float32
    ) * math.sqrt(tiles_all / (stations * green_index.shape[0]))
    summed = lax.psum(tile_spectra, "blk")
    point_share = TP // lax.axis_size("blk")
    points = blk_index * point_share + jnp.arange(point_share, dtype=jnp.int32)
    tile_image = jnp.dot(
        summed, mode_table(freq_ids, points, TILE_SIDE), precision=lax.Precision.HIGHEST
    ) / math.sqrt(F)
    return lax.psum_scatter(tile_image, "src", scatter_dimension=0, tiled=True)

LANES = 128
BOTH = ("blk", "src")
HIGHEST = lax.Precision.HIGHEST
NT_DIMS = (((1,), (1,)), ((), ()))
TN_DIMS = (((0,), (0,)), ((), ()))
VMEM_BYTES = 20 * 1024 * 1024
PARTS_TYPE = jnp.bfloat16


def split_bf16(values):
    high = values.astype(jnp.bfloat16)
    low = (values - high.astype(np.float32)).astype(jnp.bfloat16)
    return high, low


def forward_tables(n_src, n_blk):
    steps = NT // LANES
    rows = np.arange(steps)
    angle = 2 * np.pi / steps * ((rows[:, None] * rows[None, :]) % steps)
    first = np.concatenate([np.cos(angle), -np.sin(angle)], axis=0).astype(np.float32)
    first = np.concatenate(split_bf16(first), axis=0)
    lanes = np.arange(LANES)
    angle = 2 * np.pi / NT * ((lanes[:, None] * lanes[None, :]) % NT)
    twiddle = np.stack([np.cos(angle), -np.sin(angle)]).astype(np.float32)
    devices = np.arange(n_src * n_blk)
    block = devices % n_src * n_blk + devices // n_src
    angle = 2 * np.pi / steps * ((block[:, None] * lanes[None, :]) % steps)
    cos, sin = np.cos(angle), np.sin(angle)
    third = np.concatenate(
        [np.concatenate([cos, sin], axis=1), np.concatenate([-sin, cos], axis=1)], axis=0
    )
    third = split_bf16((third / math.sqrt(NT)).astype(np.float32))
    return first, twiddle, np.concatenate(third, axis=0)


def mode_tables(n_src, n_blk, scale):
    side = np.arange(TILE_SIDE)
    angle = 2 * np.pi / TILE_SIDE * ((side[:, None] * side[None, :]) % TILE_SIDE)
    cos, sin = np.cos(angle), np.sin(angle)
    low = np.zeros((2, 2, TILE_SIDE, 2, 2, TILE_SIDE))
    for parity in range(2):
        low[0, parity, :, parity, 0] = cos
        low[0, parity, :, parity, 1] = sin
        low[1, parity, :, parity, 0] = -sin
        low[1, parity, :, parity, 1] = cos
    low = low.reshape(4 * TILE_SIDE, 4 * TILE_SIDE) * scale
    devices = np.arange(n_src * n_blk)
    block = np.stack(
        [devices % n_src * n_blk + ((devices // n_src) ^ other) for other in range(2)], axis=1
    )
    high_freqs = block[..., None] * 2 + np.arange(2)
    angle = 2 * np.pi / TILE_SIDE * ((side[:, None, None, None] * high_freqs[None]) % TILE_SIDE)
    part = np.stack([np.cos(angle), -np.sin(angle)], axis=-1).reshape(
        n_blk, TILE_SIDE // n_blk, n_src * n_blk, 2, 4
    )
    high = np.zeros((n_blk, 2, TILE_SIDE // n_blk, n_src * n_blk, 2, 2, 4))
    for half in range(2):
        high[:, half, :, :, :, half] = part
    high = high.reshape(n_blk, 2 * TILE_SIDE // n_blk, 16 * n_src * n_blk)
    high = split_bf16((high / math.sqrt(F)).astype(np.float32))
    low = np.concatenate(split_bf16(low.astype(np.float32)), axis=1)
    return low, np.concatenate(high, axis=1)


def spectra_kernel(n_src, *refs):
    pieces = refs[:n_src]
    first_ref, twiddle_ref, third_ref, out_ref, samples, reals, imags = refs[n_src:]
    stations, local = pieces[1].shape
    src_index = lax.axis_index("src")
    per_src = local // LANES
    steps = per_src * n_src
    count = third_ref.shape[0] // 4
    first = first_ref[...]
    for k in range(n_src):
        start = (src_index ^ k) * per_src
        for a in range(per_src):
            samples[pl.ds(start + a, stations, stride=steps), :] = pieces[k][
                :, a * LANES : (a + 1) * LANES
            ].astype(jnp.float32)
    twiddle_real, twiddle_imag = twiddle_ref[0], twiddle_ref[1]
    third = third_ref[...]
    for station in range(0, stations, 2):
        rows = jnp.concatenate(
            [samples[(station + h) * steps : (station + h + 1) * steps, :] for h in range(2)], axis=1
        ).astype(jnp.bfloat16)
        parts = jnp.dot(first, rows, preferred_element_type=jnp.float32)
        reals_here = parts[:steps] + parts[2 * steps : 3 * steps]
        imags_here = parts[steps : 2 * steps] + parts[3 * steps :]
        turned = []
        for h in range(2):
            at = slice(h * LANES, (h + 1) * LANES)
            real = jnp.concatenate([reals_here[:, at]] * (LANES // steps), axis=0)
            imag = jnp.concatenate([imags_here[:, at]] * (LANES // steps), axis=0)
            turned.append(
                jnp.concatenate(
                    [
                        real * twiddle_real - imag * twiddle_imag,
                        real * twiddle_imag + imag * twiddle_real,
                    ],
                    axis=1,
                )
            )
        turned = jnp.concatenate(turned, axis=0)
        high = turned.astype(jnp.bfloat16)
        low = (turned - high.astype(jnp.float32)).astype(jnp.bfloat16)
        result = lax.dot_general(third, high, NT_DIMS, preferred_element_type=jnp.float32)
        result = (
            result[: 2 * count]
            + result[2 * count :]
            + lax.dot_general(
                third[: 2 * count], low, NT_DIMS, preferred_element_type=jnp.float32
            )
        )
        for h in range(2):
            at = slice(h * LANES, (h + 1) * LANES)
            reals[pl.ds(station + h, count, stride=stations), :] = result[:count, at]
            imags[pl.ds(station + h, count, stride=stations), :] = result[count:, at]
    out_ref[:, :LANES] = reals[...].astype(jnp.bfloat16)
    out_ref[:, LANES:] = imags[...].astype(jnp.bfloat16)


def bank_kernel(observed_ref, green_ref, bank_ref, bank_green_ref):
    for other in range(2):
        at = pl.ds(pl.multiple_of((lax.axis_index("blk") ^ other) * LANES, LANES), LANES)
        lanes = slice(2 * other * LANES, 2 * (other + 1) * LANES)
        pair = observed_ref[:, :, at].astype(jnp.float32)
        pair = jnp.concatenate([pair[:, 0, :], pair[:, 1, :]], axis=1)
        bank_ref[:, :, lanes] = jnp.broadcast_to(
            pair[:, None, :], (pair.shape[0], 8, 2 * LANES)
        )
        pair = green_ref[:, :, at].astype(jnp.float32)
        pair = jnp.concatenate([pair[:, 0, :], pair[:, 1, :]], axis=1)
        bank_green_ref[:, lanes] = pair.astype(jnp.bfloat16)


def pick_kernel(slots, *refs):
    *packs, green_ref, spectra_ref, picked_ref, tile_ref, squares_ref = refs
    widened = spectra_ref[...].astype(jnp.float32)
    squares_ref[...] = jnp.broadcast_to(
        jnp.sum(widened * widened, axis=0, keepdims=True), squares_ref.shape
    )
    panel = picked_ref.shape[1] // slots
    green_ids = lax.broadcasted_iota(jnp.int32, (green_ref.shape[0], slots * panel), 0)
    tile_ids = lax.broadcasted_iota(jnp.int32, (tile_ref.shape[1], slots * panel), 0)
    for k, pack in enumerate(packs):
        ids = pack[panel : panel + 16, :LANES].astype(jnp.int32)
        picks, seats = (
            jnp.concatenate([ids[row + slot : row + slot + 1, :panel] for slot in range(slots)], axis=1)
            for row in (0, 8)
        )
        picked_ref[k] = lax.dot_general(
            jnp.where(picks == green_ids, 1.0, 0.0).astype(jnp.bfloat16),
            green_ref[...],
            TN_DIMS,
            preferred_element_type=jnp.float32,
        ).astype(jnp.bfloat16)
        tile_ref[k] = jnp.where(seats == tile_ids, 1.0, 0.0).astype(jnp.bfloat16)


def three_pass(values, table_ref):
    width = table_ref.shape[1] // 2
    high = values.astype(jnp.bfloat16)
    low = (values - high.astype(jnp.float32)).astype(jnp.bfloat16)
    both = jnp.dot(high, table_ref[...], preferred_element_type=jnp.float32)
    rest = jnp.dot(low, table_ref[:, :width], preferred_element_type=jnp.float32)
    return both[:, :width] + both[:, width:] + rest


def adjoint_kernel(panels, slots, n_src, chunk, *refs):
    packs = refs[:panels]
    picked_ref, tile_ref, squares_ref, bank = refs[panels : panels + 4]
    spectra_ref, other_ref, low_ref, out_ref, spectra, mixed, total = refs[panels + 4 :]
    stations = spectra_ref.shape[0]
    panel = mixed.shape[0] // panels
    class_count = bank.shape[0]
    tiles = total.shape[0]
    blk_index = lax.axis_index("blk")
    spectra[:, : 2 * LANES] = spectra_ref[...]
    spectra[:, 2 * LANES :] = other_ref[...]
    widened = other_ref[...].astype(jnp.float32)
    squares = jnp.sum(widened * widened, axis=0, keepdims=True)
    squares = jnp.concatenate([squares_ref[:1], squares], axis=1)
    lanes = [slice(part * LANES, (part + 1) * LANES) for part in range(4)]
    power = []
    for real, imag in (lanes[:2], lanes[2:]):
        power += [squares[:, real] + squares[:, imag]] * 2
    power = jnp.concatenate(power, axis=1)
    class_ids = lax.broadcasted_iota(jnp.int32, (class_count, chunk, stations), 0)
    class_ids = class_ids.astype(jnp.float32).astype(jnp.bfloat16)
    total[...] = jnp.zeros_like(total)

    def mix(place):
        for start in range(0, panel, chunk):
            rows = packs[place][start : start + chunk]
            hot = jnp.where(rows[None] == class_ids, jnp.bfloat16(1.0), jnp.bfloat16(0.0))
            grouped = jnp.dot(
                hot.reshape(class_count * chunk, stations),
                spectra[...],
                preferred_element_type=jnp.float32,
            ).reshape(class_count, chunk // 8, 8, 4 * LANES)
            at = slice(place * panel + start, place * panel + start + chunk)
            for real, imag in (lanes[:2], lanes[2:]):
                obs_real, obs_imag = bank[:, :, real][:, None], bank[:, :, imag][:, None]
                group_real, group_imag = grouped[..., real], grouped[..., imag]
                mixed[at, real] = jnp.sum(
                    obs_real * group_real - obs_imag * group_imag, axis=0
                ).reshape(chunk, LANES)
                mixed[at, imag] = jnp.sum(
                    obs_real * group_imag + obs_imag * group_real, axis=0
                ).reshape(chunk, LANES)

    def gather(place):
        at = pl.ds(pl.multiple_of(place * panel, panel), panel)
        owner = blk_index ^ (2 * place)
        own = spectra[pl.ds(pl.multiple_of(owner * panel, panel), panel), :].astype(jnp.float32)
        adjoint = (own * power - mixed[at, :]) * (1.0 / stations)
        weighted = []
        for slot in range(slots):
            picked = picked_ref[place, slot * panel : (slot + 1) * panel].astype(jnp.float32)
            row = []
            for real, imag in (lanes[:2], lanes[2:]):
                row.append(adjoint[:, real] * picked[:, real] + adjoint[:, imag] * picked[:, imag])
                row.append(adjoint[:, real] * picked[:, imag] - adjoint[:, imag] * picked[:, real])
            weighted.append(jnp.concatenate(row, axis=1).astype(jnp.bfloat16))
        total[...] += jnp.dot(
            tile_ref[place],
            jnp.concatenate(weighted, axis=0),
            preferred_element_type=jnp.float32,
        )

    for place in range(panels):
        mix(place)
    for place in range(panels):
        gather(place)
    low = [
        three_pass(total[:, at], low_ref)
        for at in (slice(0, 2 * LANES), slice(2 * LANES, 4 * LANES))
    ]
    rows = []
    for owner in range(n_src):
        for other in range(2):
            for half in range(2):
                at = owner * (tiles // n_src) + 2 * half
                for part in range(4):
                    side = slice(part * TILE_SIDE, (part + 1) * TILE_SIDE)
                    rows.append(
                        jnp.concatenate(
                            [low[other][at : at + 1, side], low[other][at + 1 : at + 2, side]], axis=1
                        )
                    )
    rows = jnp.concatenate(rows, axis=0).astype(out_ref.dtype)
    for copy in range(out_ref.shape[0] // rows.shape[0]):
        out_ref[copy * 16 * n_src : (copy + 1) * 16 * n_src, :] = rows


def image_kernel(high_ref, parts_ref, out_ref):
    high = high_ref[lax.axis_index("blk")]
    image = jnp.dot(high, parts_ref[...], preferred_element_type=jnp.float32)
    count = image.shape[0] // 2
    image = image[:count] + image[count:]
    rows = count // 2
    for tile in range(out_ref.shape[0]):
        half, side = tile // 2, tile % 2
        for row in range(rows):
            at = half * rows + row
            out_ref[tile : tile + 1, row * TILE_SIDE : (row + 1) * TILE_SIDE] = image[
                at : at + 1, side * TILE_SIDE : (side + 1) * TILE_SIDE
            ]


def swap(values, axis, distance):
    size = lax.axis_size(axis)
    return lax.ppermute(values, axis, [(i, i ^ distance) for i in range(size)])


def split_body(windows, observed, pair_class, green, green_index, tile_index):
    n_blk, n_src = lax.axis_size("blk"), lax.axis_size("src")
    src_index = lax.axis_index("src")
    panel, local = windows.shape
    stations = panel * n_blk
    slots = green_index.shape[0]
    tiles = TILE_DEV * n_src
    share = panel // n_src
    pieces = [
        lax.dynamic_slice_in_dim(windows, (src_index ^ k) * share, share, 0)
        for k in range(n_src)
    ]
    pieces = pieces[:1] + [swap(pieces[k], "src", k) for k in range(1, n_src)]

    def widen(ids):
        return jnp.pad(ids, ((0, 8 - slots), (0, stations - panel)))

    pack = jnp.concatenate([pair_class, widen(green_index), widen(tile_index)], axis=0).astype(
        jnp.bfloat16
    )
    packs = [pack] + [swap(pack, "blk", k) for k in range(2, n_blk, 2)]

    first, twiddle, third = forward_tables(n_src, n_blk)
    low, high = mode_tables(n_src, n_blk, math.sqrt(tiles / (stations * slots)))
    devices = n_blk * n_src
    params = pltpu.CompilerParams(vmem_limit_bytes=VMEM_BYTES)
    banks = pl.pallas_call(
        bank_kernel,
        out_shape=(
            jax.ShapeDtypeStruct((observed.shape[0], 8, 4 * LANES), jnp.float32),
            jax.ShapeDtypeStruct((green.shape[0], 4 * LANES), jnp.bfloat16),
        ),
        compiler_params=params,
        name="bank",
    )(observed, green)
    pieces, banks = lax.optimization_barrier((pieces, banks))
    blocks = pl.pallas_call(
        functools.partial(spectra_kernel, n_src),
        out_shape=jax.ShapeDtypeStruct((devices * share, 2 * LANES), jnp.bfloat16),
        scratch_shapes=[
            pltpu.VMEM((share * NT // LANES, LANES), jnp.float32),
            pltpu.VMEM((devices * share, LANES), jnp.float32),
            pltpu.VMEM((devices * share, LANES), jnp.float32),
        ],
        compiler_params=params,
        name="spectra",
    )(*pieces, first, twiddle, third)
    spectra = lax.all_to_all(
        blocks.reshape(devices, share, 2 * LANES), BOTH, 0, 0, tiled=True
    ).reshape(stations, 2 * LANES)
    class_count = observed.shape[0]
    panels = n_blk // 2
    spectra, packs = lax.optimization_barrier((spectra, packs))
    picked, tile, squares = pl.pallas_call(
        functools.partial(pick_kernel, slots),
        out_shape=(
            jax.ShapeDtypeStruct((panels, slots * panel, 4 * LANES), jnp.bfloat16),
            jax.ShapeDtypeStruct((panels, tiles, slots * panel), jnp.bfloat16),
            jax.ShapeDtypeStruct((8, 2 * LANES), jnp.float32),
        ),
        compiler_params=params,
        name="pick",
    )(*packs, banks[1], spectra)
    parts = pl.pallas_call(
        functools.partial(adjoint_kernel, panels, slots, n_src, 16),
        out_shape=jax.ShapeDtypeStruct((16 * devices, 2 * TILE_SIDE), PARTS_TYPE),
        scratch_shapes=[
            pltpu.VMEM((stations, 4 * LANES), jnp.bfloat16),
            pltpu.VMEM((panels * panel, 4 * LANES), jnp.float32),
            pltpu.VMEM((tiles, 4 * LANES), jnp.float32),
        ],
        compiler_params=params,
        name="adjoint",
    )(*packs, picked, tile, squares, banks[0], spectra, swap(spectra, "blk", 1), low)
    parts = lax.all_to_all(
        parts.reshape(devices, 16, 2 * TILE_SIDE), BOTH, 0, 0, tiled=True
    ).reshape(16 * devices, 2 * TILE_SIDE)
    return pl.pallas_call(
        image_kernel,
        out_shape=jax.ShapeDtypeStruct((TILE_DEV, TP // n_blk), jnp.float32),
        compiler_params=params,
        name="image",
    )(high, parts)


def solution(mesh):
    in_specs = (
        P("blk", "src"),
        P(None, None, "src"),
        P("blk", None),
        P(None, None, "src"),
        P(None, "blk"),
        P(None, "blk"),
    )
    out_specs = P("src", "blk")
    whole_lanes = mesh.size * LANES == F
    body = split_body if whole_lanes else general_body
    return jax.shard_map(body, mesh=mesh, in_specs=in_specs, out_specs=out_specs, check_vma=False)
```
